128 devices in a mesh: circ: 8 (over z_lo, y), span: 16 (over z_hi, x, core).
Axes of the slice: x: 4, y: 4, z: 4 (z_hi: 2, z_lo: 2; z = z_hi * 2 + z_lo), core: 2. Of those that a mesh axis runs over, the one named last changes fastest.
Arguments:
- elem_rows: bfloat16 [80, 98304], P(None, ('circ', 'span')), may hold values from -6 to 6
- coupling: bfloat16 [48, 80, 80, 2048], P('circ', None, None, 'span')
- inverses: bfloat16 [48, 80, 80, 2048], P('circ', None, None, 'span'), may hold values from -0.625 to 0.625
- send_rows: int32 [128, 128, 12], P(('circ', 'span')), may hold values from 0 to 767, as said below
- recv_cells: int32 [128, 128, 12], P(('circ', 'span')), may hold values from 0 to 767, as said below
- slot_counts: int32 [128, 128], P(('circ', 'span')), may hold values from 0 to 12, as said below
Outputs:
- corrections: float32 [80, 98304], P(None, ('circ', 'span'))
The draws below stay inside these ranges and needn't reach their ends.
Inputs may be any that keep to these rules, and one draw needn't show every extreme that they name: `send_rows`: each source's filled slots name each of its 768 rows exactly once, each owner's filled slots name each of its 768 cells exactly once; unfilled slots hold 0. `recv_cells`: as send_rows, for the owners' cells. `slot_counts`: every owner's counts sum to 768, and so do every source's; some pair fills all 12 slots.
All inputs are finite; a program needn't handle non-finite values.
Results may differ from the reference program's by a relative error of at most 0.0003.
Values may be sent and summed in bfloat16 or wider, within the bound.
No kernel may reach another device: no remote copies, remote signals or barrier semaphores. Data moves between devices by JAX's collectives and lax.ppermute only.
A program may use at most 128 MiB of HBM per device.

```python
import jax
import jax.numpy as jnp
from jax import lax

W = 80
CPD = 6
NLINE = 128
CELLS = 768
CAP = 12
CIRCUIT_ZONES = 48
OVERALL_STRANDS = 2048
ROWS = 98304
N_CIRC = 8
N_SPAN = 16
DEVICES = 128


def routing_tables(key):
    key_order, key_mags, key_label, key_rows, key_cells = jax.random.split(jax.random.fold_in(key, 7), 5)
    base = CELLS // DEVICES
    half = DEVICES // 2
    order = jax.random.permutation(key_order, DEVICES)
    magnitudes = jax.random.randint(key_mags, (half,), 0, base + 1).astype(jnp.int32)
    magnitudes = magnitudes.at[0].set(base)
    offsets = jnp.zeros((DEVICES,), jnp.int32).at[order[:half]].set(magnitudes).at[order[half:]].set(-magnitudes)
    relabel = jax.random.permutation(key_label, DEVICES)
    source_index = jnp.arange(DEVICES, dtype=jnp.int32)[:, None]
    target_index = jnp.arange(DEVICES, dtype=jnp.int32)[None, :]
    counts = (base + offsets[(relabel[target_index] - source_index) % DEVICES]).astype(jnp.int32)
    slot_index = jnp.arange(CAP, dtype=jnp.int32)[None, None, :]
    row_perms = jax.vmap(lambda sub: jax.random.permutation(sub, CELLS))(jax.random.split(key_rows, DEVICES)).astype(jnp.int32)
    starts = jnp.cumsum(counts, axis=1) - counts
    places = jnp.clip(starts[:, :, None] + slot_index, 0, CELLS - 1)
    picked = jax.vmap(lambda table, where_at: table[where_at])(row_perms, places)
    send_table = jnp.where(slot_index < counts[:, :, None], picked, 0).astype(jnp.int32)
    owner_counts = jnp.transpose(counts)
    cell_perms = jax.vmap(lambda sub: jax.random.permutation(sub, CELLS))(jax.random.split(key_cells, DEVICES)).astype(jnp.int32)
    owner_starts = jnp.cumsum(owner_counts, axis=1) - owner_counts
    owner_places = jnp.clip(owner_starts[:, :, None] + slot_index, 0, CELLS - 1)
    owner_picked = jax.vmap(lambda table, where_at: table[where_at])(cell_perms, owner_places)
    recv_table = jnp.where(slot_index < owner_counts[:, :, None], owner_picked, 0).astype(jnp.int32)
    return (send_table, recv_table, owner_counts)


def draw_send_rows(key, part):
    return routing_tables(key)[0]


def draw_recv_cells(key, part):
    return routing_tables(key)[1]


def draw_slot_counts(key, part):
    return routing_tables(key)[2]


def draw_coupling(key, part):
    random_coefficient_stream, random_drawn_attenuation, random_exponent_choice, random_steep_attenuation, random_jump_choice = jax.random.split(jax.random.fold_in(key, 11), 5)
    entries = jax.random.normal(random_coefficient_stream, (CIRCUIT_ZONES, W, W, OVERALL_STRANDS), jnp.float32) / jnp.sqrt(W * 1.0)
    slow = jax.random.bernoulli(random_drawn_attenuation, 0.5, (OVERALL_STRANDS,))
    gentle = jax.random.uniform(random_exponent_choice, (OVERALL_STRANDS,), jnp.float32, 0.0, 0.5)
    strong = jax.random.uniform(random_steep_attenuation, (OVERALL_STRANDS,), jnp.float32, CIRCUIT_ZONES / 12.0, CIRCUIT_ZONES / 6.0)
    decay = jnp.where(slow, gentle, strong)
    attenuation_exponent = jnp.exp(-decay / CIRCUIT_ZONES)
    jump_places_chosen = jax.random.randint(random_jump_choice, (2, OVERALL_STRANDS), 0, CIRCUIT_ZONES)
    zone_ordinal_labels = jnp.arange(CIRCUIT_ZONES, dtype=jnp.int32)[:, None]
    jump_families = jnp.where(zone_ordinal_labels == jump_places_chosen[0][None, :], 0.75, 1.0) * jnp.where(zone_ordinal_labels == jump_places_chosen[1][None, :], 0.75, 1.0)
    magnitude_ratios = attenuation_exponent[None, :] * jump_families
    return (entries * magnitude_ratios[:, None, None, :]).astype(jnp.bfloat16)


def block_levels(key, shape, cuts, smallest, top_value):
    level = 1.0
    for dim, parts in cuts:
        heights = jax.random.uniform(jax.random.fold_in(jax.random.fold_in(key, 6), dim), (parts,), jnp.float32, smallest / len(cuts), top_value / len(cuts))
        level = level * jnp.repeat(jnp.exp(heights), shape[dim] // parts).reshape((-1,) + (1,) * (len(shape) - 1 - dim))
    return level


def scatter_about(stream_key, dims, width, most, cuts=(), kind=jnp.bfloat16):
    gain = block_levels(stream_key, dims, cuts, -0.22, 0.18) if cuts else 1.0
    values = jax.random.normal(stream_key, dims, jnp.float32) * width * gain
    return jnp.minimum(jnp.maximum(values, -most), most).astype(kind)


def setup_inputs(seed: int = 0) -> dict:
    arg_keys = jax.random.split(jax.random.key(seed), 7)
    return {
        "elem_rows": scatter_about(arg_keys[0], (W, ROWS), 1.0, 6.0, ((1, 128),)),
        "coupling": draw_coupling(jax.random.fold_in(arg_keys[6], 71), 0),
        "inverses": scatter_about(arg_keys[2], (CIRCUIT_ZONES, W, W, OVERALL_STRANDS), W ** -0.5, 0.625, ((0, 8), (3, 16))),
        "send_rows": draw_send_rows(jax.random.fold_in(arg_keys[6], 71), 0),
        "recv_cells": draw_recv_cells(jax.random.fold_in(arg_keys[6], 71), 0),
        "slot_counts": draw_slot_counts(jax.random.fold_in(arg_keys[6], 71), 0),
    }


def line_turn(coupling, inverses, line_res, incoming):
    def advance(current, position):
        forcing = jnp.einsum('ijn,jn->in', inverses[position].astype(jnp.float32), line_res[position], precision=lax.Precision.HIGHEST)
        moved = jnp.einsum('ijn,jn->in', coupling[position].astype(jnp.float32), current, precision=lax.Precision.HIGHEST)
        following = forcing + moved
        return following, following
    return lax.scan(advance, incoming, jnp.arange(CIRCUIT_ZONES, dtype=jnp.int32))


def reference(elem_rows, coupling, inverses, send_rows, recv_cells, slot_counts):
    slot_index = jnp.arange(CAP, dtype=jnp.int32)
    source_index = jnp.arange(DEVICES, dtype=jnp.int32)
    filled = slot_index[None, None, :] < jnp.transpose(slot_counts)[:, :, None]
    source_cols = (source_index[:, None, None] * CELLS + send_rows).astype(jnp.int32)
    owner_cells = jnp.transpose(recv_cells, (1, 0, 2))
    target_cols = (source_index[None, :, None] * CELLS + owner_cells).astype(jnp.int32)
    dropped = jnp.where(filled, target_cols, ROWS).astype(jnp.int32)
    line_rows = jnp.zeros((W, ROWS), jnp.bfloat16).at[:, dropped.reshape(-1)].set(elem_rows[:, source_cols.reshape(-1)], mode="drop")
    shaped = line_rows.reshape(W, N_CIRC, N_SPAN, CPD, NLINE)
    line_res = jnp.transpose(shaped, (1, 3, 0, 2, 4)).reshape(CIRCUIT_ZONES, W, OVERALL_STRANDS).astype(jnp.float32)
    nothing = jnp.zeros((W, OVERALL_STRANDS), jnp.float32)
    loop_last, unused = line_turn(coupling, inverses, line_res, nothing)
    unused_end, solved = line_turn(coupling, inverses, line_res, loop_last)
    solved = jnp.transpose(solved.reshape(N_CIRC, CPD, W, N_SPAN, NLINE), (2, 0, 3, 1, 4)).reshape(W, ROWS)
    values = solved[:, jnp.clip(target_cols, 0, ROWS - 1).reshape(-1)]
    back_cols = jnp.where(filled, source_cols, ROWS).astype(jnp.int32)
    return jnp.zeros((W, ROWS), jnp.float32).at[:, back_cols.reshape(-1)].set(values, mode="drop")
```

```python
import functools

import jax
import jax.numpy as jnp
from jax import lax
from jax.experimental import pallas as pl
from jax.experimental.pallas import tpu as pltpu
from jax.sharding import PartitionSpec as P

FEATURES = 80
SEGMENT = 6
LINES = 128
CELLS = SEGMENT * LINES
PEERS = 128
SLOTS = 12
PAIRS = SLOTS // 2
ROWS = 8
MAIN = 64
TAIL = FEATURES - MAIN
N_CIRC = 8

IN_VMEM = pl.BlockSpec(memory_space=pltpu.VMEM)
F32 = jnp.float32
BF16 = jnp.bfloat16


def params(megabytes):
    return pltpu.CompilerParams(vmem_limit_bytes=megabytes * 2**20)


def fold_sublanes(parts, row):
    upper = row < 4
    fours = []
    for k in range(4):
        a, b = parts[k], parts[k + 4]
        fours.append(jnp.where(upper, a, b) + pltpu.roll(jnp.where(upper, b, a), 4, 0))
    even_pair = (row & 2) == 0
    twos = []
    for k in range(2):
        a, b = fours[k], fours[k + 2]
        twos.append(jnp.where(even_pair, a + pltpu.roll(a, 6, 0), b + pltpu.roll(b, 2, 0)))
    even = (row & 1) == 0
    a, b = twos
    return jnp.where(even, a + pltpu.roll(a, 7, 0), b + pltpu.roll(b, 1, 0))


def matvec(blocks_ref, position, vector, row):
    result = []
    for group in range(FEATURES // 8):
        parts = []
        for k in range(8):
            terms = blocks_ref[position, group * 8 + k].astype(F32) * vector
            total = terms[0:8]
            for j in range(8, FEATURES, 8):
                total = total + terms[j : j + 8]
            parts.append(total)
        result.append(fold_sublanes(parts, row))
    return jnp.concatenate(result, axis=0)


def sublane_ids():
    return lax.broadcasted_iota(jnp.int32, (8, LINES), 0)


def columns(table):
    padded = jnp.concatenate([table, jnp.full((16 - SLOTS, PEERS), -1, jnp.int32)], axis=0)
    return jnp.transpose(padded)


def one_hot(index, first):
    place = lax.broadcasted_iota(jnp.int32, (PEERS, CELLS), 1)
    return jnp.concatenate(
        [
            jnp.where(index[:, 2 * pair + first : 2 * pair + first + 1] == place, 1.0, 0.0).astype(BF16)
            for pair in range(PAIRS)
        ],
        axis=0,
    )


def across(a, b):
    return lax.dot_general(a, b, (((1,), (1,)), ((), ())), preferred_element_type=F32)


def down(a, b):
    return lax.dot_general(a, b, (((0,), (0,)), ((), ())), preferred_element_type=F32)


def spread(rows, offset):
    tail_at = 128 + (0 if offset == 0 else TAIL)
    parts = [rows[:MAIN], rows[MAIN:]]
    gaps = [offset, tail_at - offset - MAIN, 256 - tail_at - TAIL]
    filled = []
    for gap, part in zip(gaps, parts + [None]):
        if gap:
            filled.append(jnp.zeros((gap, CELLS), BF16))
        if part is not None:
            filled.append(part)
    return jnp.concatenate(filled, axis=0)


def pack(pieces, index, store):
    packed = 0.0
    for first, offset in ((0, 0), (1, MAIN)):
        hot = one_hot(index, first)
        for piece in pieces:
            packed = packed + across(hot, spread(piece, offset))
    tails = []
    for pair in range(PAIRS):
        rows = packed[pair * PEERS : (pair + 1) * PEERS]
        store(pair, rows[:, :128])
        tail = rows[:, 128:]
        shift = 2 * TAIL * (pair % 4)
        tails.append(pltpu.roll(tail, shift, 1) if shift else tail)
    store(6, tails[0] + tails[1] + tails[2] + tails[3])
    store(7, tails[4] + tails[5])


def unpack(load, index, pieces):
    lane = lax.broadcasted_iota(jnp.int32, (PEERS, 128), 1)
    last = (load(6), load(7))
    total = 0.0
    for first in range(2):
        slots = []
        for pair in range(PAIRS):
            rows = load(pair)
            if first:
                rows = pltpu.roll(rows, MAIN, 1)
            shift = (MAIN - 2 * TAIL * (pair % 4) - TAIL * first) % 128
            tail = last[pair // 4]
            tail = pltpu.roll(tail, shift, 1) if shift else tail
            slots.append(jnp.where(lane < MAIN, rows, jnp.where(lane < FEATURES, tail, 0.0)))
        slots = jnp.concatenate(slots, axis=0)
        hot = one_hot(index, first)
        for _ in range(pieces):
            part = slots.astype(BF16)
            total = total + down(part, hot)
            slots = slots - part.astype(F32)
    return total[:FEATURES]


def pack_rows_kernel(rows_ref, send_ref, out_ref, wide):
    def store(r, block):
        wide[pl.ds(r, PEERS, stride=ROWS), :] = block

    pack([rows_ref[...]], columns(send_ref[...]), store)
    out_ref[...] = wide[...].astype(BF16)


def forcing_kernel(arrived_ref, cells_ref, counts_ref, inverses_ref, forcing_ref, wide, lines):
    wide[...] = arrived_ref[...].astype(F32)
    slot = lax.broadcasted_iota(jnp.int32, (SLOTS, PEERS), 0)
    cells = jnp.where(slot < counts_ref[...], cells_ref[...], -1)
    found = unpack(lambda r: wide[pl.ds(r, PEERS, stride=ROWS), :], columns(cells), 1)
    for position in range(SEGMENT):
        lines[position] = found[:, position * LINES : (position + 1) * LINES]
    row = sublane_ids()

    @pl.loop(0, SEGMENT)
    def _(position):
        forcing_ref[position] = matvec(inverses_ref, position, lines[position], row)


def hop_kernel(hop, *refs):
    if hop == 0:
        coupling_ref, forcing_ref, end_ref = refs
        state_ref = solved_ref = None
    elif hop < N_CIRC:
        state_ref, coupling_ref, forcing_ref, end_ref = refs
        solved_ref = None
    elif hop < 2 * N_CIRC - 1:
        state_ref, coupling_ref, forcing_ref, end_ref, solved_ref = refs
    else:
        state_ref, coupling_ref, forcing_ref, solved_ref = refs
        end_ref = None

    @pl.when(lax.axis_index("circ") == hop % N_CIRC)
    def _():
        row = sublane_ids()

        def step(position, state):
            state = forcing_ref[position] + matvec(coupling_ref, position, state, row)
            if solved_ref is not None:
                solved_ref[position] = state
            return state

        if hop == 0:
            state = lax.fori_loop(1, SEGMENT, step, forcing_ref[0])
        else:
            state = lax.fori_loop(0, SEGMENT, step, state_ref[...])
        if end_ref is not None:
            end_ref[...] = state


def return_pack_kernel(solved_ref, cells_ref, counts_ref, out_ref):
    def store(r, block):
        out_ref[pl.ds(r, PEERS, stride=ROWS), :] = block

    slot = lax.broadcasted_iota(jnp.int32, (SLOTS, PEERS), 0)
    cells = jnp.where(slot < counts_ref[...], cells_ref[...], -1)
    rest = jnp.concatenate([solved_ref[position] for position in range(SEGMENT)], axis=1)
    high = rest.astype(BF16)
    low = (rest - high.astype(F32)).astype(BF16)
    pack([high, low], columns(cells), store)


def return_kernel(arrived_ref, send_ref, out_ref):
    out_ref[...] = unpack(
        lambda r: arrived_ref[pl.ds(r, PEERS, stride=ROWS), :], columns(send_ref[...]), 2
    )


def vmem(x):
    return pltpu.with_memory_space_constraint(x, pltpu.VMEM)


def exchange(rows):
    blocks = rows.reshape(PEERS, ROWS, 128)
    moved = lax.all_to_all(blocks, ("circ", "span"), split_axis=0, concat_axis=0, tiled=True)
    return moved.reshape(PEERS * ROWS, 128)


def local(elem_rows, coupling, inverses, send_rows, recv_cells, slot_counts):
    send = jnp.transpose(send_rows[0])
    cells = jnp.transpose(recv_cells[0])
    packed_rows = (PEERS * ROWS, 128)
    state_shape = jax.ShapeDtypeStruct((FEATURES, LINES), F32)
    forcing_shape = jax.ShapeDtypeStruct((SEGMENT, FEATURES, LINES), F32)
    outgoing = pl.pallas_call(
        pack_rows_kernel,
        out_shape=jax.ShapeDtypeStruct(packed_rows, BF16),
        in_specs=[IN_VMEM] * 2,
        out_specs=IN_VMEM,
        scratch_shapes=[pltpu.VMEM(packed_rows, F32)],
        compiler_params=params(16),
        name="pack_rows",
    )(elem_rows, send)
    arrived = exchange(outgoing)
    coupling = vmem(coupling)
    forcing = pl.pallas_call(
        forcing_kernel,
        out_shape=forcing_shape,
        in_specs=[IN_VMEM] * 4,
        out_specs=IN_VMEM,
        scratch_shapes=[
            pltpu.VMEM(packed_rows, F32),
            pltpu.VMEM((SEGMENT, FEATURES, LINES), F32),
        ],
        compiler_params=params(16),
        name="forcing",
    )(arrived, cells, slot_counts, vmem(inverses))

    state = None
    for hop in range(2 * N_CIRC):
        operands = ([] if hop == 0 else [state]) + [coupling, vmem(forcing)]
        second, final = hop >= N_CIRC, hop == 2 * N_CIRC - 1
        shapes = ([] if final else [state_shape]) + ([forcing_shape] if second else [])
        results = pl.pallas_call(
            functools.partial(hop_kernel, hop),
            out_shape=shapes,
            in_specs=[IN_VMEM] * len(operands),
            out_specs=[IN_VMEM] * len(shapes),
            input_output_aliases={len(operands) - 1: len(shapes) - 1} if second else {},
            compiler_params=params(8),
            name="hop",
        )(*operands)
        if second:
            forcing = results[-1]
        if not final:
            here = hop % N_CIRC
            state = lax.ppermute(results[0], "circ", [(here, (here + 1) % N_CIRC)])

    returning = pl.pallas_call(
        return_pack_kernel,
        out_shape=jax.ShapeDtypeStruct(packed_rows, F32),
        in_specs=[IN_VMEM] * 3,
        out_specs=IN_VMEM,
        compiler_params=params(16),
        name="return_pack",
    )(forcing, cells, slot_counts)
    returned = exchange(returning)
    return pl.pallas_call(
        return_kernel,
        out_shape=jax.ShapeDtypeStruct((FEATURES, CELLS), F32),
        in_specs=[IN_VMEM] * 2,
        out_specs=IN_VMEM,
        compiler_params=params(16),
        name="return_rows",
    )(returned, send)


def solution(mesh):
    return jax.shard_map(
        local,
        mesh=mesh,
        in_specs=(
            P(None, ("circ", "span")),
            P("circ", None, None, "span"),
            P("circ", None, None, "span"),
            P(("circ", "span"), None, None),
            P(("circ", "span"), None, None),
            P(("circ", "span"), None),
        ),
        out_specs=P(None, ("circ", "span")),
        check_vma=False,
    )
```

```python
import functools

import jax
import jax.numpy as jnp
from jax import lax
from jax.experimental import pallas as pl
from jax.experimental.pallas import tpu as pltpu
from jax.sharding import PartitionSpec as P

FEATURES = 80
SEGMENT = 6
LINES = 128
CELLS = SEGMENT * LINES
PEERS = 128
SLOTS = 12
PAIRS = SLOTS // 2
ROWS = 8
MAIN = 64
TAIL = FEATURES - MAIN
N_CIRC = 8
HALF = FEATURES // 2
LANES = 128
SIDE = LANES // 2

IN_VMEM = pl.BlockSpec(memory_space=pltpu.VMEM)
F32 = jnp.float32
BF16 = jnp.bfloat16


def params(megabytes):
    return pltpu.CompilerParams(vmem_limit_bytes=megabytes * 2**20)


def fold_sublanes(parts, row):
    upper = row < 4
    fours = []
    for k in range(4):
        a, b = parts[k], parts[k + 4]
        fours.append(jnp.where(upper, a, b) + pltpu.roll(jnp.where(upper, b, a), 4, 0))
    even_pair = (row & 2) == 0
    twos = []
    for k in range(2):
        a, b = fours[k], fours[k + 2]
        twos.append(jnp.where(even_pair, a + pltpu.roll(a, 6, 0), b + pltpu.roll(b, 2, 0)))
    even = (row & 1) == 0
    a, b = twos
    return jnp.where(even, a + pltpu.roll(a, 7, 0), b + pltpu.roll(b, 1, 0))


def matvec(blocks_ref, position, vector, row):
    result = []
    for group in range(blocks_ref.shape[1] // 8):
        parts = []
        for k in range(8):
            terms = blocks_ref[position, group * 8 + k].astype(F32) * vector
            total = terms[0:8]
            for j in range(8, FEATURES, 8):
                total = total + terms[j : j + 8]
            parts.append(total)
        result.append(fold_sublanes(parts, row))
    return jnp.concatenate(result, axis=0)


def sublane_ids():
    return lax.broadcasted_iota(jnp.int32, (8, LINES), 0)


def columns(table):
    padded = jnp.concatenate([table, jnp.full((16 - SLOTS, PEERS), -1, jnp.int32)], axis=0)
    return jnp.transpose(padded)


def one_hot(index, first):
    place = lax.broadcasted_iota(jnp.int32, (PEERS, CELLS), 1)
    return jnp.concatenate(
        [
            jnp.where(index[:, 2 * pair + first : 2 * pair + first + 1] == place, 1.0, 0.0).astype(BF16)
            for pair in range(PAIRS)
        ],
        axis=0,
    )


def across(a, b):
    return lax.dot_general(a, b, (((1,), (1,)), ((), ())), preferred_element_type=F32)


def down(a, b):
    return lax.dot_general(a, b, (((0,), (0,)), ((), ())), preferred_element_type=F32)


def spread(rows, offset):
    tail_at = 128 + (0 if offset == 0 else TAIL)
    parts = [rows[:MAIN], rows[MAIN:]]
    gaps = [offset, tail_at - offset - MAIN, 256 - tail_at - TAIL]
    filled = []
    for gap, part in zip(gaps, parts + [None]):
        if gap:
            filled.append(jnp.zeros((gap, CELLS), BF16))
        if part is not None:
            filled.append(part)
    return jnp.concatenate(filled, axis=0)


def swap(x):
    return pltpu.roll(x, SIDE, 1)


def left(rows):
    return lax.broadcasted_iota(jnp.int32, (rows, LANES), 1) < SIDE


def pack(pieces, hots, store):
    packed = 0.0
    for hot, offset in zip(hots, (0, MAIN)):
        for piece in pieces:
            packed = packed + across(hot, spread(piece, offset))
    tails = []
    for pair in range(PAIRS):
        rows = packed[pair * PEERS : (pair + 1) * PEERS]
        store(pair, rows[:, :128])
        tail = rows[:, 128:]
        shift = 2 * TAIL * (pair % 4)
        tails.append(pltpu.roll(tail, shift, 1) if shift else tail)
    store(6, tails[0] + tails[1] + tails[2] + tails[3])
    store(7, tails[4] + tails[5])


def unpack(load, hots, pieces):
    lane = lax.broadcasted_iota(jnp.int32, (PEERS, 128), 1)
    last = (load(6), load(7))
    total = 0.0
    for first in range(2):
        slots = []
        for pair in range(PAIRS):
            rows = load(pair)
            if first:
                rows = pltpu.roll(rows, MAIN, 1)
            shift = (MAIN - 2 * TAIL * (pair % 4) - TAIL * first) % 128
            tail = last[pair // 4]
            tail = pltpu.roll(tail, shift, 1) if shift else tail
            slots.append(jnp.where(lane < MAIN, rows, jnp.where(lane < FEATURES, tail, 0.0)))
        slots = jnp.concatenate(slots, axis=0)
        hot = hots[first]
        for _ in range(pieces):
            part = slots.astype(BF16)
            total = total + down(part, hot)
            slots = slots - part.astype(F32)
    return total[:FEATURES]


def pack_rows_kernel(rows_ref, send_ref, out_ref, wide):
    def store(r, block):
        wide[pl.ds(r, PEERS, stride=ROWS), :] = block

    index = columns(send_ref[...])
    pack([rows_ref[...]], (one_hot(index, 0), one_hot(index, 1)), store)
    out_ref[...] = wide[...].astype(BF16)


def bundle_kernel(coupling_ref, bundle_a, bundle_b):
    on_left = left(HALF)

    @pl.loop(0, coupling_ref.shape[2])
    def _(i):
        low = coupling_ref[0, 0, i].astype(F32)
        high = coupling_ref[0, 1, i].astype(F32)
        for ref, a, b in ((bundle_a, low, swap(high)), (bundle_b, swap(low), high)):
            same = jnp.where(on_left, a[:HALF], b[HALF:])
            cross = jnp.where(on_left, a[HALF:], b[:HALF])
            ref[0, i] = jnp.concatenate([same, cross], axis=0).astype(BF16)


def forcing_kernel(
    arrived_ref, cells_ref, counts_ref, inverses_hbm, bundle_hbm,
    forcing_a, forcing_b, even_ref, odd_ref, bundle_ref,
    wide, lines, inverses_ref, sems, bundle_sem,
):
    copies = [
        pltpu.make_async_copy(inverses_hbm.at[p], inverses_ref.at[p], sems.at[p])
        for p in range(SEGMENT)
    ]
    for copy in copies:
        copy.start()
    bundle_copy = pltpu.make_async_copy(bundle_hbm, bundle_ref, bundle_sem)
    bundle_copy.start()
    wide[...] = arrived_ref[...].astype(F32)
    slot = lax.broadcasted_iota(jnp.int32, (SLOTS, PEERS), 0)
    index = columns(jnp.where(slot < counts_ref[...], cells_ref[...], -1))
    hots = one_hot(index, 0), one_hot(index, 1)
    even_ref[...], odd_ref[...] = hots
    found = unpack(lambda r: wide[pl.ds(r, PEERS, stride=ROWS), :], hots, 1)
    for p in range(SEGMENT):
        lines[p] = found[:, p * LINES : (p + 1) * LINES]
    row = sublane_ids()
    on_left = left(HALF)
    for p in range(SEGMENT):
        copies[p].wait()
        forcing = matvec(inverses_ref, p, lines[p], row)
        low, high = forcing[:HALF], forcing[HALF:]
        forcing_a[p] = jnp.where(on_left, low, swap(high))
        forcing_b[p] = jnp.where(on_left, swap(low), high)
    bundle_copy.wait()


def advance(coupling_ref, forcing_ref, first, state, record=None):
    row = sublane_ids()

    def step(position, state):
        both = jnp.concatenate([state, swap(state)], axis=0)
        state = forcing_ref[position] + matvec(coupling_ref, position, both, row)
        if record is not None:
            record[position] = state
        return state

    return lax.fori_loop(first, SEGMENT, step, state)


def here(hop):
    return lax.axis_index("circ") == hop % N_CIRC


def first_hop_kernel(bundle_hbm, coupling_ref, forcing_ref, end_ref, bundle_ref, sem):
    copy = pltpu.make_async_copy(bundle_hbm, bundle_ref, sem)
    copy.start()

    @pl.when(here(0))
    def _():
        end_ref[...] = advance(coupling_ref, forcing_ref, 1, forcing_ref[0])

    copy.wait()


def hop_kernel(hop, *refs):
    *state_refs, coupling_ref, forcing_ref, end_ref = refs

    @pl.when(here(hop))
    def _():
        if state_refs:
            end_ref[...] = advance(coupling_ref, forcing_ref, 0, state_refs[0][...])
        else:
            end_ref[...] = advance(coupling_ref, forcing_ref, 1, forcing_ref[0])


def final_kernel(*refs):
    *state_refs, coupling_ref, forcing_ref, solved_ref = refs
    state = state_refs[0][...]
    for ref in state_refs[1:]:
        state = state + ref[...]
    advance(coupling_ref, forcing_ref, 0, state, solved_ref)


def return_pack_kernel(solved_a, solved_b, even_ref, odd_ref, out_ref):
    def store(r, block):
        out_ref[pl.ds(r, PEERS, stride=ROWS), :] = block

    on_left = left(HALF)
    cells = []
    for position in range(SEGMENT):
        a, b = solved_a[position], solved_b[position]
        low = jnp.where(on_left, a, swap(b))
        high = jnp.where(on_left, swap(a), b)
        cells.append(jnp.concatenate([low, high], axis=0))
    rest = jnp.concatenate(cells, axis=1)
    high = rest.astype(BF16)
    low = (rest - high.astype(F32)).astype(BF16)
    pack([high, low], (even_ref[...], odd_ref[...]), store)


def return_kernel(arrived_ref, send_ref, out_ref):
    index = columns(send_ref[...])
    out_ref[...] = unpack(
        lambda r: arrived_ref[pl.ds(r, PEERS, stride=ROWS), :],
        (one_hot(index, 0), one_hot(index, 1)),
        2,
    )


def vmem(x):
    return pltpu.with_memory_space_constraint(x, pltpu.VMEM)


def hbm(x):
    return pltpu.with_memory_space_constraint(x, pltpu.HBM)


def exchange(rows):
    blocks = rows.reshape(PEERS, ROWS, 128)
    moved = lax.all_to_all(blocks, ("circ", "span"), split_axis=0, concat_axis=0, tiled=True)
    return moved.reshape(PEERS * ROWS, 128)


def local(elem_rows, coupling, inverses, send_rows, recv_cells, slot_counts):
    send = jnp.transpose(send_rows[0])
    cells = jnp.transpose(recv_cells[0])
    packed_rows = (PEERS * ROWS, LANES)
    hot_shape = jax.ShapeDtypeStruct((PAIRS * PEERS, CELLS), BF16)
    bundle_shape = jax.ShapeDtypeStruct((SEGMENT, HALF, FEATURES, LANES), BF16)
    state_shape = jax.ShapeDtypeStruct((HALF, LANES), F32)
    forcing_shape = jax.ShapeDtypeStruct((SEGMENT, HALF, LANES), F32)
    in_hbm = pl.BlockSpec(memory_space=pltpu.HBM)
    outgoing = pl.pallas_call(
        pack_rows_kernel,
        out_shape=jax.ShapeDtypeStruct(packed_rows, BF16),
        in_specs=[IN_VMEM] * 2,
        out_specs=IN_VMEM,
        scratch_shapes=[pltpu.VMEM(packed_rows, F32)],
        compiler_params=params(16),
        name="pack_rows",
    )(elem_rows, send)
    arrived = exchange(outgoing)
    split = 2
    bundles = pl.pallas_call(
        bundle_kernel,
        out_shape=[bundle_shape] * 2,
        grid=(SEGMENT, split),
        in_specs=[
            pl.BlockSpec((1, 2, HALF // split, FEATURES, LANES), lambda p, k: (p, 0, k, 0, 0))
        ],
        out_specs=[pl.BlockSpec((1, HALF // split, FEATURES, LANES), lambda p, k: (p, k, 0, 0))] * 2,
        compiler_params=params(16),
        cost_estimate=pl.CostEstimate(flops=0, bytes_accessed=4 * coupling.size, transcendentals=0),
        name="bundle",
    )(hbm(coupling.reshape(SEGMENT, 2, HALF, FEATURES, LANES)))
    *forcings, even, odd, bundle_a = pl.pallas_call(
        forcing_kernel,
        out_shape=[forcing_shape] * 2 + [hot_shape] * 2 + [bundle_shape],
        in_specs=[IN_VMEM] * 3 + [in_hbm] * 2,
        out_specs=[IN_VMEM] * 5,
        scratch_shapes=[
            pltpu.VMEM(packed_rows, F32),
            pltpu.VMEM((SEGMENT, FEATURES, LINES), F32),
            pltpu.VMEM(inverses.shape, BF16),
            pltpu.SemaphoreType.DMA((SEGMENT,)),
            pltpu.SemaphoreType.DMA,
        ],
        compiler_params=params(24),
        name="forcing",
    )(arrived, cells, slot_counts, hbm(inverses), hbm(bundles[0]))
    even, odd = vmem(even), vmem(odd)
    bundle_a = vmem(bundle_a)
    forcings = [vmem(forcing) for forcing in forcings]
    end_a, bundle_b = pl.pallas_call(
        first_hop_kernel,
        out_shape=[state_shape, bundle_shape],
        in_specs=[in_hbm] + [IN_VMEM] * 2,
        out_specs=[IN_VMEM] * 2,
        scratch_shapes=[pltpu.SemaphoreType.DMA],
        compiler_params=params(8),
        name="hop_a",
    )(hbm(bundles[1]), bundle_a, forcings[0])
    bundles = [bundle_a, vmem(bundle_b)]

    def sweep(side, kernel, states, shape, name):
        operands = [*states, bundles[side], forcings[side]]
        return pl.pallas_call(
            kernel,
            out_shape=shape,
            in_specs=[IN_VMEM] * len(operands),
            out_specs=IN_VMEM,
            compiler_params=params(8),
            cost_estimate=pl.CostEstimate(
                flops=2 * 10**6, bytes_accessed=2 * bundle_shape.size, transcendentals=0
            ),
            name=name + "ab"[side],
        )(*operands)

    arrivals = ([], [])
    for hop in range(2 * N_CIRC - 1):
        for side in range(2):
            if hop == 0 and side == 0:
                end = end_a
            else:
                end = sweep(
                    side, functools.partial(hop_kernel, hop), arrivals[side][-1:], state_shape, "hop_"
                )
            pair = (hop % N_CIRC, (hop + 1) % N_CIRC)
            arrivals[side].append(lax.ppermute(end, "circ", [pair]))
    solved = [
        sweep(side, final_kernel, arrivals[side][N_CIRC - 1 :], forcing_shape, "final_")
        for side in range(2)
    ]

    returning = pl.pallas_call(
        return_pack_kernel,
        out_shape=jax.ShapeDtypeStruct(packed_rows, F32),
        in_specs=[IN_VMEM] * 4,
        out_specs=IN_VMEM,
        compiler_params=params(16),
        name="return_pack",
    )(*solved, even, odd)
    returned = exchange(returning)
    return pl.pallas_call(
        return_kernel,
        out_shape=jax.ShapeDtypeStruct((FEATURES, CELLS), F32),
        in_specs=[IN_VMEM] * 2,
        out_specs=IN_VMEM,
        compiler_params=params(16),
        name="return_rows",
    )(returned, send)


def solution(mesh):
    return jax.shard_map(
        local,
        mesh=mesh,
        in_specs=(
            P(None, ("circ", "span")),
            P("circ", None, None, "span"),
            P("circ", None, None, "span"),
            P(("circ", "span"), None, None),
            P(("circ", "span"), None, None),
            P(("circ", "span"), None),
        ),
        out_specs=P(None, ("circ", "span")),
        check_vma=False,
    )
```

```python
import functools

import jax
import jax.numpy as jnp
from jax import lax
from jax.experimental import pallas as pl
from jax.experimental.pallas import tpu as pltpu
from jax.sharding import PartitionSpec as P

FEATURES = 80
SEGMENT = 6
LINES = 128
CELLS = SEGMENT * LINES
PEERS = 128
SLOTS = 12
PAIRS = SLOTS // 2
ROWS = 8
MAIN = 64
TAIL = FEATURES - MAIN
N_CIRC = 8
HALF = FEATURES // 2
LANES = 128
SIDE = LANES // 2

IN_VMEM = pl.BlockSpec(memory_space=pltpu.VMEM)
F32 = jnp.float32
BF16 = jnp.bfloat16


def params(megabytes):
    return pltpu.CompilerParams(vmem_limit_bytes=megabytes * 2**20)


def fold_sublanes(parts, row):
    upper = row < 4
    fours = []
    for k in range(4):
        a, b = parts[k], parts[k + 4]
        fours.append(jnp.where(upper, a, b) + pltpu.roll(jnp.where(upper, b, a), 4, 0))
    even_pair = (row & 2) == 0
    twos = []
    for k in range(2):
        a, b = fours[k], fours[k + 2]
        twos.append(jnp.where(even_pair, a + pltpu.roll(a, 6, 0), b + pltpu.roll(b, 2, 0)))
    even = (row & 1) == 0
    a, b = twos
    return jnp.where(even, a + pltpu.roll(a, 7, 0), b + pltpu.roll(b, 1, 0))


def matvec(blocks_ref, position, vector, row):
    result = []
    for group in range(blocks_ref.shape[1] // 8):
        parts = []
        for k in range(8):
            terms = blocks_ref[position, group * 8 + k].astype(F32) * vector
            total = terms[0:8]
            for j in range(8, FEATURES, 8):
                total = total + terms[j : j + 8]
            parts.append(total)
        result.append(fold_sublanes(parts, row))
    return jnp.concatenate(result, axis=0)


def sublane_ids():
    return lax.broadcasted_iota(jnp.int32, (8, LINES), 0)


def columns(table):
    padded = jnp.concatenate([table, jnp.full((16 - SLOTS, PEERS), -1, jnp.int32)], axis=0)
    return jnp.transpose(padded)


def one_hot(index, first):
    place = lax.broadcasted_iota(jnp.int32, (PEERS, CELLS), 1)
    return jnp.concatenate(
        [
            jnp.where(index[:, 2 * pair + first : 2 * pair + first + 1] == place, 1.0, 0.0).astype(BF16)
            for pair in range(PAIRS)
        ],
        axis=0,
    )


def across(a, b):
    return lax.dot_general(a, b, (((1,), (1,)), ((), ())), preferred_element_type=F32)


def down(a, b):
    return lax.dot_general(a, b, (((0,), (0,)), ((), ())), preferred_element_type=F32)


def spread(rows, offset):
    tail_at = 128 + (0 if offset == 0 else TAIL)
    parts = [rows[:MAIN], rows[MAIN:]]
    gaps = [offset, tail_at - offset - MAIN, 256 - tail_at - TAIL]
    filled = []
    for gap, part in zip(gaps, parts + [None]):
        if gap:
            filled.append(jnp.zeros((gap, CELLS), BF16))
        if part is not None:
            filled.append(part)
    return jnp.concatenate(filled, axis=0)


def swap(x):
    return pltpu.roll(x, SIDE, 1)


def left(rows):
    return lax.broadcasted_iota(jnp.int32, (rows, LANES), 1) < SIDE


def pack(pieces, hots, store):
    packed = 0.0
    for hot, offset in zip(hots, (0, MAIN)):
        for piece in pieces:
            packed = packed + across(hot, spread(piece, offset))
    tails = []
    for pair in range(PAIRS):
        rows = packed[pair * PEERS : (pair + 1) * PEERS]
        store(pair, rows[:, :128])
        tail = rows[:, 128:]
        shift = 2 * TAIL * (pair % 4)
        tails.append(pltpu.roll(tail, shift, 1) if shift else tail)
    store(6, tails[0] + tails[1] + tails[2] + tails[3])
    store(7, tails[4] + tails[5])


def unpack(load, hots, pieces):
    lane = lax.broadcasted_iota(jnp.int32, (PEERS, 128), 1)
    last = (load(6), load(7))
    total = 0.0
    for first in range(2):
        slots = []
        for pair in range(PAIRS):
            rows = load(pair)
            if first:
                rows = pltpu.roll(rows, MAIN, 1)
            shift = (MAIN - 2 * TAIL * (pair % 4) - TAIL * first) % 128
            tail = last[pair // 4]
            tail = pltpu.roll(tail, shift, 1) if shift else tail
            slots.append(jnp.where(lane < MAIN, rows, jnp.where(lane < FEATURES, tail, 0.0)))
        slots = jnp.concatenate(slots, axis=0)
        hot = hots[first]
        for _ in range(pieces):
            part = slots.astype(BF16)
            total = total + down(part, hot)
            slots = slots - part.astype(F32)
    return total[:FEATURES]


def pack_rows_kernel(rows_hbm, send_ref, out_ref, wide, rows_ref, sem):
    copy = pltpu.make_async_copy(rows_hbm, rows_ref, sem)
    copy.start()

    def store(r, block):
        wide[pl.ds(r, PEERS, stride=ROWS), :] = block

    index = columns(send_ref[...].reshape(SLOTS, PEERS))
    hots = one_hot(index, 0), one_hot(index, 1)
    copy.wait()
    pack([rows_ref[...]], hots, store)
    out_ref[...] = wide[...].astype(BF16)


def bundle_kernel(coupling_ref, bundle_a, bundle_b):
    on_left = left(FEATURES)

    @pl.loop(0, coupling_ref.shape[2], unroll=4)
    def _(i):
        low = coupling_ref[0, 0, i]
        high = swap(coupling_ref[0, 1, i].astype(F32)).astype(BF16)
        bundle_a[0, i] = jnp.where(on_left, low, high)
        bundle_b[0, i] = jnp.where(on_left, high, low)


def advance(side, coupling_ref, forcing_ref, first, state, record=None):
    row = sublane_ids()
    on_left = left(HALF)

    def step(position, state):
        moved = swap(state)
        both = [jnp.where(on_left, state, moved), jnp.where(on_left, moved, state)]
        both = jnp.concatenate(both[::-1] if side else both, axis=0)
        state = forcing_ref[position] + matvec(coupling_ref, position, both, row)
        if record is not None:
            record[position] = state
        return state

    if callable(first):
        for position in range(1, SEGMENT):
            first(position)
            state = step(position, state)
        return state
    return lax.fori_loop(first, SEGMENT, step, state)


def forcing_kernel(
    arrived_ref, cells_ref, counts_ref, inverses_hbm, bundle_hbm,
    forcing_a, forcing_b, even_ref, odd_ref, bundle_ref, end_ref,
    wide, lines, inverses_ref, sems, bundle_sems,
):
    copies = [
        pltpu.make_async_copy(inverses_hbm.at[p], inverses_ref.at[p], sems.at[p])
        for p in range(SEGMENT)
    ]
    for copy in copies:
        copy.start()
    bundle_copies = [
        pltpu.make_async_copy(bundle_hbm.at[p], bundle_ref.at[p], bundle_sems.at[p])
        for p in range(SEGMENT)
    ]
    for copy in bundle_copies[1:] + bundle_copies[:1]:
        copy.start()
    wide[...] = arrived_ref[...].astype(F32)
    slot = lax.broadcasted_iota(jnp.int32, (SLOTS, PEERS), 0)
    index = columns(jnp.where(slot < counts_ref[...], cells_ref[...].reshape(SLOTS, PEERS), -1))
    hots = one_hot(index, 0), one_hot(index, 1)
    even_ref[...], odd_ref[...] = hots
    found = unpack(lambda r: wide[pl.ds(r, PEERS, stride=ROWS), :], hots, 1)
    for p in range(SEGMENT):
        lines[p] = found[:, p * LINES : (p + 1) * LINES]
    row = sublane_ids()
    on_left = left(HALF)
    for p in range(SEGMENT):
        copies[p].wait()
        forcing = matvec(inverses_ref, p, lines[p], row)
        low, high = forcing[:HALF], swap(forcing[HALF:])
        forcing_a[p] = jnp.where(on_left, low, high)
        forcing_b[p] = jnp.where(on_left, high, low)
    end_ref[...] = advance(
        0, bundle_ref, forcing_a, lambda p: bundle_copies[p].wait(), forcing_a[0]
    )
    bundle_copies[0].wait()


def here(hop):
    return lax.axis_index("circ") == hop % N_CIRC


def first_hop_kernel(bundle_hbm, forcing_ref, end_ref, bundle_ref, sems):
    copies = [
        pltpu.make_async_copy(bundle_hbm.at[p], bundle_ref.at[p], sems.at[p])
        for p in range(SEGMENT)
    ]
    for copy in copies[1:] + copies[:1]:
        copy.start()
    end_ref[...] = advance(1, bundle_ref, forcing_ref, lambda p: copies[p].wait(), forcing_ref[0])
    copies[0].wait()


def hop_kernel(hop, side, state_ref, coupling_ref, forcing_ref, end_ref):
    @pl.when(here(hop))
    def _():
        end_ref[...] = advance(side, coupling_ref, forcing_ref, 0, state_ref[...])


def final_kernel(side, *refs):
    *state_refs, coupling_ref, forcing_ref, solved_ref = refs
    state = state_refs[0][...]
    for ref in state_refs[1:]:
        state = state + ref[...]
    advance(side, coupling_ref, forcing_ref, 0, state, solved_ref)


def return_pack_kernel(solved_a, solved_b, even_ref, odd_ref, out_ref):
    def store(r, block):
        out_ref[pl.ds(r, PEERS, stride=ROWS), :] = block

    on_left = left(HALF)
    cells = []
    for position in range(SEGMENT):
        a, b = solved_a[position], solved_b[position]
        low = jnp.where(on_left, a, b)
        high = swap(jnp.where(on_left, b, a))
        cells.append(jnp.concatenate([low, high], axis=0))
    rest = jnp.concatenate(cells, axis=1)
    high = rest.astype(BF16)
    low = (rest - high.astype(F32)).astype(BF16)
    pack([high, low], (even_ref[...], odd_ref[...]), store)


def return_kernel(arrived_ref, send_ref, out_ref):
    index = columns(send_ref[...].reshape(SLOTS, PEERS))
    out_ref[...] = unpack(
        lambda r: arrived_ref[pl.ds(r, PEERS, stride=ROWS), :],
        (one_hot(index, 0), one_hot(index, 1)),
        2,
    )


def vmem(x):
    return pltpu.with_memory_space_constraint(x, pltpu.VMEM)


def hbm(x):
    return pltpu.with_memory_space_constraint(x, pltpu.HBM)


def exchange(rows):
    blocks = rows.reshape(PEERS, ROWS, 128)
    moved = lax.all_to_all(blocks, ("circ", "span"), split_axis=0, concat_axis=0, tiled=True)
    return moved.reshape(PEERS * ROWS, 128)


def local(elem_rows, coupling, inverses, send_rows, recv_cells, slot_counts):
    send = jnp.transpose(send_rows, (2, 0, 1))
    cells = jnp.transpose(recv_cells, (2, 0, 1))
    packed_rows = (PEERS * ROWS, LANES)
    hot_shape = jax.ShapeDtypeStruct((PAIRS * PEERS, CELLS), BF16)
    bundle_shape = jax.ShapeDtypeStruct((SEGMENT, HALF, FEATURES, LANES), BF16)
    state_shape = jax.ShapeDtypeStruct((HALF, LANES), F32)
    forcing_shape = jax.ShapeDtypeStruct((SEGMENT, HALF, LANES), F32)
    in_hbm = pl.BlockSpec(memory_space=pltpu.HBM)
    outgoing = pl.pallas_call(
        pack_rows_kernel,
        out_shape=jax.ShapeDtypeStruct(packed_rows, BF16),
        in_specs=[in_hbm, IN_VMEM],
        out_specs=IN_VMEM,
        scratch_shapes=[
            pltpu.VMEM(packed_rows, F32),
            pltpu.VMEM(elem_rows.shape, BF16),
            pltpu.SemaphoreType.DMA,
        ],
        compiler_params=params(16),
        name="pack_rows",
    )(hbm(elem_rows), send)
    arrived = exchange(outgoing)
    split = 2
    bundles = pl.pallas_call(
        bundle_kernel,
        out_shape=[pltpu.HBM(bundle_shape.shape, BF16)] * 2,
        grid=(SEGMENT, split),
        in_specs=[
            pl.BlockSpec((1, 2, HALF // split, FEATURES, LANES), lambda p, k: (p, 0, k, 0, 0))
        ],
        out_specs=[pl.BlockSpec((1, HALF // split, FEATURES, LANES), lambda p, k: (p, k, 0, 0))] * 2,
        compiler_params=params(16),
        cost_estimate=pl.CostEstimate(flops=0, bytes_accessed=4 * coupling.size, transcendentals=0),
        name="bundle",
    )(hbm(coupling.reshape(SEGMENT, 2, HALF, FEATURES, LANES)))
    *forcings, even, odd, bundle_a, end_a = pl.pallas_call(
        forcing_kernel,
        out_shape=[forcing_shape] * 2 + [hot_shape] * 2 + [bundle_shape, state_shape],
        in_specs=[IN_VMEM] * 3 + [in_hbm] * 2,
        out_specs=[IN_VMEM] * 6,
        scratch_shapes=[
            pltpu.VMEM(packed_rows, F32),
            pltpu.VMEM((SEGMENT, FEATURES, LINES), F32),
            pltpu.VMEM(inverses.shape, BF16),
            pltpu.SemaphoreType.DMA((SEGMENT,)),
            pltpu.SemaphoreType.DMA((SEGMENT,)),
        ],
        compiler_params=params(24),
        name="forcing",
    )(arrived, cells, slot_counts, hbm(inverses), hbm(bundles[0]))
    even, odd = vmem(even), vmem(odd)
    forcings = [vmem(forcing) for forcing in forcings]
    end_b, bundle_b = pl.pallas_call(
        first_hop_kernel,
        out_shape=[state_shape, bundle_shape],
        in_specs=[in_hbm, IN_VMEM],
        out_specs=[IN_VMEM] * 2,
        scratch_shapes=[pltpu.SemaphoreType.DMA((SEGMENT,))],
        compiler_params=params(8),
        name="first_hop",
    )(hbm(bundles[1]), forcings[1])
    bundles = [vmem(bundle_a), vmem(bundle_b)]

    def sweep(side, kernel, states, shape, name):
        operands = [*states, bundles[side], forcings[side]]
        return pl.pallas_call(
            kernel,
            out_shape=shape,
            in_specs=[IN_VMEM] * len(operands),
            out_specs=IN_VMEM,
            compiler_params=params(8),
            cost_estimate=pl.CostEstimate(
                flops=2 * 10**6, bytes_accessed=2 * bundle_shape.size, transcendentals=0
            ),
            name=name + "ab"[side],
        )(*operands)

    arrivals = ([], [])
    for hop in range(2 * N_CIRC - 1):
        for side in range(2):
            end = (end_a, end_b)[side]
            if hop:
                kernel = functools.partial(hop_kernel, hop, side)
                end = sweep(side, kernel, arrivals[side][-1:], state_shape, "hop_")
            pair = (hop % N_CIRC, (hop + 1) % N_CIRC)
            arrivals[side].append(lax.ppermute(end, "circ", [pair]))
    solved = [
        sweep(side, functools.partial(final_kernel, side), arrivals[side][N_CIRC - 1 :], forcing_shape, "final_")
        for side in range(2)
    ]

    returning = pl.pallas_call(
        return_pack_kernel,
        out_shape=jax.ShapeDtypeStruct(packed_rows, F32),
        in_specs=[IN_VMEM] * 4,
        out_specs=IN_VMEM,
        compiler_params=params(16),
        name="return_pack",
    )(*solved, even, odd)
    returned = exchange(returning)
    return pl.pallas_call(
        return_kernel,
        out_shape=jax.ShapeDtypeStruct((FEATURES, CELLS), F32),
        in_specs=[IN_VMEM] * 2,
        out_specs=IN_VMEM,
        compiler_params=params(16),
        name="return_rows",
    )(returned, send)


def solution(mesh):
    return jax.shard_map(
        local,
        mesh=mesh,
        in_specs=(
            P(None, ("circ", "span")),
            P("circ", None, None, "span"),
            P("circ", None, None, "span"),
            P(("circ", "span"), None, None),
            P(("circ", "span"), None, None),
            P(("circ", "span"), None),
        ),
        out_specs=P(None, ("circ", "span")),
        check_vma=False,
    )
```

```python
import functools

import jax
import jax.numpy as jnp
from jax import lax
from jax.experimental import pallas as pl
from jax.experimental.pallas import tpu as pltpu
from jax.sharding import PartitionSpec as P

FEATURES = 80
SEGMENT = 6
LINES = 128
CELLS = SEGMENT * LINES
PEERS = 128
SLOTS = 12
PAIRS = SLOTS // 2
ROWS = 8
MAIN = 64
TAIL = FEATURES - MAIN
N_CIRC = 8
HALF = FEATURES // 2
LANES = 128
SIDE = LANES // 2

IN_VMEM = pl.BlockSpec(memory_space=pltpu.VMEM)
F32 = jnp.float32
BF16 = jnp.bfloat16


def params(megabytes):
    return pltpu.CompilerParams(vmem_limit_bytes=megabytes * 2**20)


def fold_sublanes(parts, row):
    upper = row < 4
    fours = []
    for k in range(4):
        a, b = parts[k], parts[k + 4]
        fours.append(jnp.where(upper, a, b) + pltpu.roll(jnp.where(upper, b, a), 4, 0))
    even_pair = (row & 2) == 0
    twos = []
    for k in range(2):
        a, b = fours[k], fours[k + 2]
        twos.append(jnp.where(even_pair, a + pltpu.roll(a, 6, 0), b + pltpu.roll(b, 2, 0)))
    even = (row & 1) == 0
    a, b = twos
    return jnp.where(even, a + pltpu.roll(a, 7, 0), b + pltpu.roll(b, 1, 0))


def matvec(blocks_ref, position, vector, row):
    result = []
    for group in range(blocks_ref.shape[1] // 8):
        parts = []
        for k in range(8):
            terms = blocks_ref[position, group * 8 + k].astype(F32) * vector
            total = terms[0:8]
            for j in (*range(16, FEATURES, 16), *range(8, FEATURES, 16)):
                total = total + terms[j : j + 8]
            parts.append(total)
        result.append(fold_sublanes(parts, row))
    return jnp.concatenate(result, axis=0)


def sublane_ids():
    return lax.broadcasted_iota(jnp.int32, (8, LINES), 0)


def columns(table):
    padded = jnp.concatenate([table, jnp.full((16 - SLOTS, PEERS), -1, jnp.int32)], axis=0)
    return jnp.transpose(padded)


def one_hot(index, first):
    place = lax.broadcasted_iota(jnp.int32, (PEERS, CELLS), 1)
    return jnp.concatenate(
        [
            jnp.where(index[:, 2 * pair + first : 2 * pair + first + 1] == place, 1.0, 0.0).astype(BF16)
            for pair in range(PAIRS)
        ],
        axis=0,
    )


def across(a, b):
    return lax.dot_general(a, b, (((1,), (1,)), ((), ())), preferred_element_type=F32)


def down(a, b):
    return lax.dot_general(a, b, (((0,), (0,)), ((), ())), preferred_element_type=F32)


def spread(rows, offset):
    tail_at = 128 + (0 if offset == 0 else TAIL)
    parts = [rows[:MAIN], rows[MAIN:]]
    gaps = [offset, tail_at - offset - MAIN, 256 - tail_at - TAIL]
    filled = []
    for gap, part in zip(gaps, parts + [None]):
        if gap:
            filled.append(jnp.zeros((gap, CELLS), BF16))
        if part is not None:
            filled.append(part)
    return jnp.concatenate(filled, axis=0)


def swap(x):
    return pltpu.roll(x, SIDE, 1)


def left(rows):
    return lax.broadcasted_iota(jnp.int32, (rows, LANES), 1) < SIDE


def pack(pieces, hots, store):
    packed = 0.0
    for hot, offset in zip(hots, (0, MAIN)):
        for piece in pieces:
            packed = packed + across(hot, spread(piece, offset))
    tails = []
    for pair in range(PAIRS):
        rows = packed[pair * PEERS : (pair + 1) * PEERS]
        store(pair, rows[:, :128])
        tail = rows[:, 128:]
        shift = 2 * TAIL * (pair % 4)
        tails.append(pltpu.roll(tail, shift, 1) if shift else tail)
    store(6, tails[0] + tails[1] + tails[2] + tails[3])
    store(7, tails[4] + tails[5])


def unpack(load, hots, pieces):
    lane = lax.broadcasted_iota(jnp.int32, (PEERS, 128), 1)
    last = (load(6), load(7))
    total = 0.0
    for first in range(2):
        slots = []
        for pair in range(PAIRS):
            rows = load(pair)
            if first:
                rows = pltpu.roll(rows, MAIN, 1)
            shift = (MAIN - 2 * TAIL * (pair % 4) - TAIL * first) % 128
            tail = last[pair // 4]
            tail = pltpu.roll(tail, shift, 1) if shift else tail
            slots.append(jnp.where(lane < MAIN, rows, jnp.where(lane < FEATURES, tail, 0.0)))
        slots = jnp.concatenate(slots, axis=0)
        hot = hots[first]
        for _ in range(pieces):
            part = slots.astype(BF16)
            total = total + down(part, hot)
            slots = slots - part.astype(F32)
    return total[:FEATURES]


def pack_rows_kernel(rows_hbm, send_ref, out_ref, wide, rows_ref, sem):
    copy = pltpu.make_async_copy(rows_hbm, rows_ref, sem)
    copy.start()

    def store(r, block):
        wide[pl.ds(r, PEERS, stride=ROWS), :] = block

    index = columns(send_ref[...].reshape(SLOTS, PEERS))
    hots = one_hot(index, 0), one_hot(index, 1)
    copy.wait()
    pack([rows_ref[...]], hots, store)
    out_ref[...] = wide[...].astype(BF16)


def bundle_kernel(coupling_hbm, bundle_a_hbm, bundle_b_hbm, whole, bundle_a, bundle_b, sems):
    fetch, put_a, put_b = [
        [pltpu.make_async_copy(src.at[p], dst.at[p], sems.at[k, p]) for p in range(SEGMENT)]
        for k, (src, dst) in enumerate(
            ((coupling_hbm, whole), (bundle_a, bundle_a_hbm), (bundle_b, bundle_b_hbm))
        )
    ]
    for copy in fetch:
        copy.start()
    on_left = left(FEATURES)
    for p in range(SEGMENT):
        fetch[p].wait()

        @pl.loop(0, HALF // 8)
        def _(block):
            for k in range(8):
                low = whole[p, block * 16 + k]
                high = whole[p, block * 16 + 8 + k].astype(F32)
                high = jnp.concatenate(
                    [swap(high[j * 8 : j * 8 + 8]) for i in range(HALF // 8) for j in (2 * i + 1, 2 * i)],
                    axis=0,
                ).astype(BF16)
                bundle_a[p, block * 8 + k] = jnp.where(on_left, low, high)
                bundle_b[p, block * 8 + k] = jnp.where(on_left, high, low)

        put_a[p].start()
        put_b[p].start()
    for copy in put_a + put_b:
        copy.wait()


def blocks8(x, odd):
    return jnp.concatenate([x[j * 8 : j * 8 + 8] for j in range(odd, FEATURES // 8, 2)], axis=0)


def advance(coupling_ref, forcing_ref, first, state, record=None):
    row = sublane_ids()

    def step(position, state):
        own = [state[j : j + 8] for j in range(0, HALF, 8)]
        both = jnp.concatenate([x for block in own for x in (block, swap(block))], axis=0)
        state = forcing_ref[position] + matvec(coupling_ref, position, both, row)
        if record is not None:
            record[position] = state
        return state

    if callable(first):
        for position in range(1, SEGMENT):
            first(position)
            state = step(position, state)
        return state
    return lax.fori_loop(first, SEGMENT, step, state)


def forcing_kernel(
    arrived_ref, cells_ref, counts_ref, inverses_hbm, bundle_hbm,
    forcing_a, forcing_b, even_ref, odd_ref, bundle_ref, end_ref,
    wide, lines, inverses_ref, sems, bundle_sems,
):
    copies = [
        pltpu.make_async_copy(inverses_hbm.at[p], inverses_ref.at[p], sems.at[p])
        for p in range(SEGMENT)
    ]
    for copy in copies:
        copy.start()
    bundle_copies = [
        pltpu.make_async_copy(bundle_hbm.at[p], bundle_ref.at[p], bundle_sems.at[p])
        for p in range(SEGMENT)
    ]
    for copy in bundle_copies[1:] + bundle_copies[:1]:
        copy.start()
    wide[...] = arrived_ref[...].astype(F32)
    slot = lax.broadcasted_iota(jnp.int32, (SLOTS, PEERS), 0)
    index = columns(jnp.where(slot < counts_ref[...], cells_ref[...].reshape(SLOTS, PEERS), -1))
    hots = one_hot(index, 0), one_hot(index, 1)
    even_ref[...], odd_ref[...] = hots
    found = unpack(lambda r: wide[pl.ds(r, PEERS, stride=ROWS), :], hots, 1)
    for p in range(SEGMENT):
        lines[p] = found[:, p * LINES : (p + 1) * LINES]
    row = sublane_ids()
    on_left = left(HALF)
    for p in range(SEGMENT):
        copies[p].wait()
        forcing = matvec(inverses_ref, p, lines[p], row)
        low, high = blocks8(forcing, 0), swap(blocks8(forcing, 1))
        forcing_a[p] = jnp.where(on_left, low, high)
        forcing_b[p] = jnp.where(on_left, high, low)
    end_ref[...] = advance(
        bundle_ref, forcing_a, lambda p: bundle_copies[p].wait(), forcing_a[0]
    )
    bundle_copies[0].wait()


def here(hop):
    return lax.axis_index("circ") == hop % N_CIRC


def first_hop_kernel(bundle_hbm, forcing_ref, end_ref, bundle_ref, sems):
    copies = [
        pltpu.make_async_copy(bundle_hbm.at[p], bundle_ref.at[p], sems.at[p])
        for p in range(SEGMENT)
    ]
    for copy in copies[1:] + copies[:1]:
        copy.start()
    end_ref[...] = advance(bundle_ref, forcing_ref, lambda p: copies[p].wait(), forcing_ref[0])
    copies[0].wait()


def hop_kernel(hop, state_ref, coupling_ref, forcing_ref, end_ref):
    @pl.when(here(hop))
    def _():
        end_ref[...] = advance(coupling_ref, forcing_ref, 0, state_ref[...])


def final_kernel(*refs):
    *state_refs, coupling_ref, forcing_ref, solved_ref = refs
    state = state_refs[0][...]
    for ref in state_refs[1:]:
        state = state + ref[...]
    advance(coupling_ref, forcing_ref, 0, state, solved_ref)


def return_pack_kernel(solved_a, solved_b, even_ref, odd_ref, out_ref):
    def store(r, block):
        out_ref[pl.ds(r, PEERS, stride=ROWS), :] = block

    on_left = left(HALF)
    cells = []
    for position in range(SEGMENT):
        a, b = solved_a[position], solved_b[position]
        low = jnp.where(on_left, a, b)
        high = swap(jnp.where(on_left, b, a))
        blocks = [x[j : j + 8] for j in range(0, HALF, 8) for x in (low, high)]
        cells.append(jnp.concatenate(blocks, axis=0))
    rest = jnp.concatenate(cells, axis=1)
    high = rest.astype(BF16)
    low = (rest - high.astype(F32)).astype(BF16)
    pack([high, low], (even_ref[...], odd_ref[...]), store)


def return_kernel(arrived_ref, send_ref, out_ref):
    index = columns(send_ref[...].reshape(SLOTS, PEERS))
    out_ref[...] = unpack(
        lambda r: arrived_ref[pl.ds(r, PEERS, stride=ROWS), :],
        (one_hot(index, 0), one_hot(index, 1)),
        2,
    )


def vmem(x):
    return pltpu.with_memory_space_constraint(x, pltpu.VMEM)


def hbm(x):
    return pltpu.with_memory_space_constraint(x, pltpu.HBM)


def exchange(rows):
    blocks = rows.reshape(PEERS, ROWS, 128)
    moved = lax.all_to_all(blocks, ("circ", "span"), split_axis=0, concat_axis=0, tiled=True)
    return moved.reshape(PEERS * ROWS, 128)


def local(elem_rows, coupling, inverses, send_rows, recv_cells, slot_counts):
    send = jnp.transpose(send_rows, (2, 0, 1))
    cells = jnp.transpose(recv_cells, (2, 0, 1))
    packed_rows = (PEERS * ROWS, LANES)
    hot_shape = jax.ShapeDtypeStruct((PAIRS * PEERS, CELLS), BF16)
    bundle_shape = jax.ShapeDtypeStruct((SEGMENT, HALF, FEATURES, LANES), BF16)
    state_shape = jax.ShapeDtypeStruct((HALF, LANES), F32)
    forcing_shape = jax.ShapeDtypeStruct((SEGMENT, HALF, LANES), F32)
    in_hbm = pl.BlockSpec(memory_space=pltpu.HBM)
    outgoing = pl.pallas_call(
        pack_rows_kernel,
        out_shape=jax.ShapeDtypeStruct(packed_rows, BF16),
        in_specs=[in_hbm, IN_VMEM],
        out_specs=IN_VMEM,
        scratch_shapes=[
            pltpu.VMEM(packed_rows, F32),
            pltpu.VMEM(elem_rows.shape, BF16),
            pltpu.SemaphoreType.DMA,
        ],
        compiler_params=params(16),
        name="pack_rows",
    )(hbm(elem_rows), send)
    arrived = exchange(outgoing)
    bundles = pl.pallas_call(
        bundle_kernel,
        out_shape=[pltpu.HBM(bundle_shape.shape, BF16)] * 2,
        in_specs=[in_hbm],
        out_specs=[in_hbm] * 2,
        scratch_shapes=[
            pltpu.VMEM(coupling.shape, BF16),
            pltpu.VMEM(bundle_shape.shape, BF16),
            pltpu.VMEM(bundle_shape.shape, BF16),
            pltpu.SemaphoreType.DMA((3, SEGMENT)),
        ],
        compiler_params=params(32),
        cost_estimate=pl.CostEstimate(flops=0, bytes_accessed=4 * coupling.size, transcendentals=0),
        name="bundle",
    )(hbm(coupling))
    *forcings, even, odd, bundle_a, end_a = pl.pallas_call(
        forcing_kernel,
        out_shape=[forcing_shape] * 2 + [hot_shape] * 2 + [bundle_shape, state_shape],
        in_specs=[IN_VMEM] * 3 + [in_hbm] * 2,
        out_specs=[IN_VMEM] * 6,
        scratch_shapes=[
            pltpu.VMEM(packed_rows, F32),
            pltpu.VMEM((SEGMENT, FEATURES, LINES), F32),
            pltpu.VMEM(inverses.shape, BF16),
            pltpu.SemaphoreType.DMA((SEGMENT,)),
            pltpu.SemaphoreType.DMA((SEGMENT,)),
        ],
        compiler_params=params(24),
        name="forcing",
    )(arrived, cells, slot_counts, hbm(inverses), hbm(bundles[0]))
    even, odd = vmem(even), vmem(odd)
    forcings = [vmem(forcing) for forcing in forcings]
    end_b, bundle_b = pl.pallas_call(
        first_hop_kernel,
        out_shape=[state_shape, bundle_shape],
        in_specs=[in_hbm, IN_VMEM],
        out_specs=[IN_VMEM] * 2,
        scratch_shapes=[pltpu.SemaphoreType.DMA((SEGMENT,))],
        compiler_params=params(8),
        name="first_hop",
    )(hbm(bundles[1]), forcings[1])
    bundles = [vmem(bundle_a), vmem(bundle_b)]

    def sweep(side, kernel, states, shape, name):
        operands = [*states, bundles[side], forcings[side]]
        return pl.pallas_call(
            kernel,
            out_shape=shape,
            in_specs=[IN_VMEM] * len(operands),
            out_specs=IN_VMEM,
            compiler_params=params(8),
            cost_estimate=pl.CostEstimate(
                flops=2 * 10**6, bytes_accessed=2 * bundle_shape.size, transcendentals=0
            ),
            name=name + "ab"[side],
        )(*operands)

    arrivals = ([], [])
    for hop in range(2 * N_CIRC - 1):
        for side in range(2):
            end = (end_a, end_b)[side]
            if hop:
                kernel = functools.partial(hop_kernel, hop)
                end = sweep(side, kernel, arrivals[side][-1:], state_shape, "hop_")
            pair = (hop % N_CIRC, (hop + 1) % N_CIRC)
            arrivals[side].append(lax.ppermute(end, "circ", [pair]))
    solved = [
        sweep(side, final_kernel, arrivals[side][N_CIRC - 1 :], forcing_shape, "final_")
        for side in range(2)
    ]

    returning = pl.pallas_call(
        return_pack_kernel,
        out_shape=jax.ShapeDtypeStruct(packed_rows, F32),
        in_specs=[IN_VMEM] * 4,
        out_specs=IN_VMEM,
        compiler_params=params(16),
        name="return_pack",
    )(*solved, even, odd)
    returned = exchange(returning)
    return pl.pallas_call(
        return_kernel,
        out_shape=jax.ShapeDtypeStruct((FEATURES, CELLS), F32),
        in_specs=[IN_VMEM] * 2,
        out_specs=IN_VMEM,
        compiler_params=params(16),
        name="return_rows",
    )(returned, send)


def solution(mesh):
    return jax.shard_map(
        local,
        mesh=mesh,
        in_specs=(
            P(None, ("circ", "span")),
            P("circ", None, None, "span"),
            P("circ", None, None, "span"),
            P(("circ", "span"), None, None),
            P(("circ", "span"), None, None),
            P(("circ", "span"), None),
        ),
        out_specs=P(None, ("circ", "span")),
        check_vma=False,
    )
```

```python
import functools

import jax
import jax.numpy as jnp
from jax import lax
from jax.experimental import pallas as pl
from jax.experimental.pallas import tpu as pltpu
from jax.sharding import PartitionSpec as P

FEATURES = 80
SEGMENT = 6
LINES = 128
CELLS = SEGMENT * LINES
PEERS = 128
SLOTS = 12
PAIRS = SLOTS // 2
ROWS = 8
MAIN = 64
TAIL = FEATURES - MAIN
N_CIRC = 8
HALF = FEATURES // 2
LANES = 128
SIDE = LANES // 2

IN_VMEM = pl.BlockSpec(memory_space=pltpu.VMEM)
F32 = jnp.float32
BF16 = jnp.bfloat16


def params(megabytes):
    return pltpu.CompilerParams(vmem_limit_bytes=megabytes * 2**20)


def fold_sublanes(parts, row):
    upper = row < 4
    fours = []
    for k in range(4):
        a, b = parts[k], parts[k + 4]
        fours.append(jnp.where(upper, a, b) + pltpu.roll(jnp.where(upper, b, a), 4, 0))
    even_pair = (row & 2) == 0
    twos = []
    for k in range(2):
        a, b = fours[k], fours[k + 2]
        twos.append(jnp.where(even_pair, a + pltpu.roll(a, 6, 0), b + pltpu.roll(b, 2, 0)))
    even = (row & 1) == 0
    a, b = twos
    return jnp.where(even, a + pltpu.roll(a, 7, 0), b + pltpu.roll(b, 1, 0))


def matvec(blocks_ref, position, vector, row):
    result = []
    for group in range(blocks_ref.shape[1] // 8):
        parts = []
        for k in range(8):
            terms = blocks_ref[position, group * 8 + k].astype(F32) * vector
            total = terms[0:8]
            for j in (*range(16, FEATURES, 16), *range(8, FEATURES, 16)):
                total = total + terms[j : j + 8]
            parts.append(total)
        result.append(fold_sublanes(parts, row))
    return jnp.concatenate(result, axis=0)


def sublane_ids():
    return lax.broadcasted_iota(jnp.int32, (8, LINES), 0)


def columns(table):
    padded = jnp.concatenate([table, jnp.full((16 - SLOTS, PEERS), -1, jnp.int32)], axis=0)
    return jnp.transpose(padded)


def one_hot(index, first):
    place = lax.broadcasted_iota(jnp.int32, (PEERS, CELLS), 1)
    return jnp.concatenate(
        [
            jnp.where(index[:, 2 * pair + first : 2 * pair + first + 1] == place, 1.0, 0.0).astype(BF16)
            for pair in range(PAIRS)
        ],
        axis=0,
    )


def across(a, b):
    return lax.dot_general(a, b, (((1,), (1,)), ((), ())), preferred_element_type=F32)


def down(a, b):
    return lax.dot_general(a, b, (((0,), (0,)), ((), ())), preferred_element_type=F32)


def spread(rows, offset):
    tail_at = 128 + (0 if offset == 0 else TAIL)
    parts = [rows[:MAIN], rows[MAIN:]]
    gaps = [offset, tail_at - offset - MAIN, 256 - tail_at - TAIL]
    filled = []
    for gap, part in zip(gaps, parts + [None]):
        if gap:
            filled.append(jnp.zeros((gap, CELLS), BF16))
        if part is not None:
            filled.append(part)
    return jnp.concatenate(filled, axis=0)


def swap(x):
    return pltpu.roll(x, SIDE, 1)


def left(rows):
    return lax.broadcasted_iota(jnp.int32, (rows, LANES), 1) < SIDE


def pack(pieces, hots, store):
    packed = 0.0
    for hot, offset in zip(hots, (0, MAIN)):
        for piece in pieces:
            packed = packed + across(hot, spread(piece, offset))
    tails = []
    for pair in range(PAIRS):
        rows = packed[pair * PEERS : (pair + 1) * PEERS]
        store(pair, rows[:, :128])
        tail = rows[:, 128:]
        shift = 2 * TAIL * (pair % 4)
        tails.append(pltpu.roll(tail, shift, 1) if shift else tail)
    store(6, tails[0] + tails[1] + tails[2] + tails[3])
    store(7, tails[4] + tails[5])


def unpack(load, hots, pieces):
    lane = lax.broadcasted_iota(jnp.int32, (PEERS, 128), 1)
    last = (load(6), load(7))
    total = 0.0
    for first in range(2):
        slots = []
        for pair in range(PAIRS):
            rows = load(pair)
            if first:
                rows = pltpu.roll(rows, MAIN, 1)
            shift = (MAIN - 2 * TAIL * (pair % 4) - TAIL * first) % 128
            tail = last[pair // 4]
            tail = pltpu.roll(tail, shift, 1) if shift else tail
            slots.append(jnp.where(lane < MAIN, rows, jnp.where(lane < FEATURES, tail, 0.0)))
        slots = jnp.concatenate(slots, axis=0)
        hot = hots[first]
        for _ in range(pieces):
            part = slots.astype(BF16)
            total = total + down(part, hot)
            slots = slots - part.astype(F32)
    return total[:FEATURES]


def pack_rows_kernel(rows_hbm, send_ref, out_ref, wide, rows_ref, sem):
    copy = pltpu.make_async_copy(rows_hbm, rows_ref, sem)
    copy.start()

    def store(r, block):
        wide[pl.ds(r, PEERS, stride=ROWS), :] = block

    index = columns(send_ref[...].reshape(SLOTS, PEERS))
    hots = one_hot(index, 0), one_hot(index, 1)
    copy.wait()
    pack([rows_ref[...]], hots, store)
    out_ref[...] = wide[...].astype(BF16)


def bundle_kernel(coupling_hbm, bundle_a_hbm, bundle_b_hbm, whole, bundle_a, bundle_b, sems):
    fetch, put_a, put_b = [
        [pltpu.make_async_copy(src.at[p], dst.at[p], sems.at[k, p]) for p in range(SEGMENT)]
        for k, (src, dst) in enumerate(
            ((coupling_hbm, whole), (bundle_a, bundle_a_hbm), (bundle_b, bundle_b_hbm))
        )
    ]
    for copy in fetch:
        copy.start()
    on_left = left(FEATURES)
    for p in range(SEGMENT):
        fetch[p].wait()

        @pl.loop(0, HALF // 8)
        def _(block):
            for k in range(8):
                low = whole[p, block * 16 + k]
                high = whole[p, block * 16 + 8 + k].astype(F32)
                high = jnp.concatenate(
                    [swap(high[j * 8 : j * 8 + 8]) for i in range(HALF // 8) for j in (2 * i + 1, 2 * i)],
                    axis=0,
                ).astype(BF16)
                bundle_a[p, block * 8 + k] = jnp.where(on_left, low, high)
                bundle_b[p, block * 8 + k] = jnp.where(on_left, high, low)

        put_a[p].start()
        put_b[p].start()
    for copy in put_a + put_b:
        copy.wait()


def blocks8(x, odd):
    return jnp.concatenate([x[j * 8 : j * 8 + 8] for j in range(odd, FEATURES // 8, 2)], axis=0)


def advance(coupling_ref, forcing_ref, first, state, record=None):
    row = sublane_ids()

    def step(position, state):
        own = [state[j : j + 8] for j in range(0, HALF, 8)]
        both = jnp.concatenate([x for block in own for x in (block, swap(block))], axis=0)
        state = forcing_ref[position] + matvec(coupling_ref, position, both, row)
        if record is not None:
            record[position] = state
        return state

    if callable(first):

        def waited(position, state):
            first(position)
            return step(position, state)

        return lax.fori_loop(1, SEGMENT, waited, state)
    return lax.fori_loop(first, SEGMENT, step, state, unroll=True)


def forcing_kernel(
    arrived_ref, cells_ref, counts_ref, inverses_hbm, bundle_hbm,
    forcing_a, forcing_b, even_ref, odd_ref, bundle_ref, end_ref,
    wide, lines, inverses_ref, sems, bundle_sems,
):
    def copy(p):
        return pltpu.make_async_copy(inverses_hbm.at[p], inverses_ref.at[p], sems.at[p])

    def bundle_copy(p):
        return pltpu.make_async_copy(bundle_hbm.at[p], bundle_ref.at[p], bundle_sems.at[p])

    for p in range(SEGMENT):
        copy(p).start()
    for p in range(1, SEGMENT):
        bundle_copy(p).start()
    wide[...] = arrived_ref[...].astype(F32)
    slot = lax.broadcasted_iota(jnp.int32, (SLOTS, PEERS), 0)
    index = columns(jnp.where(slot < counts_ref[...], cells_ref[...].reshape(SLOTS, PEERS), -1))
    hots = one_hot(index, 0), one_hot(index, 1)
    even_ref[...], odd_ref[...] = hots
    found = unpack(lambda r: wide[pl.ds(r, PEERS, stride=ROWS), :], hots, 1)
    for p in range(SEGMENT):
        lines[p] = found[:, p * LINES : (p + 1) * LINES]
    row = sublane_ids()
    on_left = left(HALF)

    @pl.loop(0, SEGMENT)
    def _(p):
        copy(p).wait()
        forcing = matvec(inverses_ref, p, lines[p], row)
        low, high = blocks8(forcing, 0), swap(blocks8(forcing, 1))
        forcing_a[p] = jnp.where(on_left, low, high)
        forcing_b[p] = jnp.where(on_left, high, low)
    end_ref[...] = advance(
        bundle_ref, forcing_a, lambda p: bundle_copy(p).wait(), forcing_a[0]
    )


def here(hop):
    return lax.axis_index("circ") == hop % N_CIRC


def first_hop_kernel(bundle_hbm, forcing_ref, end_ref, bundle_ref, sems):
    def copy(p):
        return pltpu.make_async_copy(bundle_hbm.at[p], bundle_ref.at[p], sems.at[p])

    for p in range(1, SEGMENT):
        copy(p).start()
    end_ref[...] = advance(bundle_ref, forcing_ref, lambda p: copy(p).wait(), forcing_ref[0])


def widen_kernel(bundle_hbm, bundle_ref, wide_ref, first, sem):
    copy = pltpu.make_async_copy(bundle_hbm.at[0], first, sem)
    copy.start()

    @pl.loop(1, SEGMENT)
    def _(p):
        @pl.loop(0, HALF, unroll=8)
        def _(i):
            wide_ref[p, i] = bundle_ref[p, i].astype(F32)

    copy.wait()

    @pl.loop(0, HALF, unroll=8)
    def _(i):
        wide_ref[0, i] = first[i].astype(F32)


def hop_kernel(hop, state_ref, coupling_ref, forcing_ref, end_ref):
    @pl.when(here(hop))
    def _():
        end_ref[...] = advance(coupling_ref, forcing_ref, 0, state_ref[...])


def final_kernel(*refs):
    *state_refs, coupling_ref, forcing_ref, solved_ref = refs
    state = state_refs[0][...]
    for ref in state_refs[1:]:
        state = state + ref[...]
    advance(coupling_ref, forcing_ref, 0, state, solved_ref)


def return_pack_kernel(solved_a, solved_b, even_ref, odd_ref, out_ref):
    def store(r, block):
        out_ref[pl.ds(r, PEERS, stride=ROWS), :] = block

    on_left = left(HALF)
    cells = []
    for position in range(SEGMENT):
        a, b = solved_a[position], solved_b[position]
        low = jnp.where(on_left, a, b)
        high = swap(jnp.where(on_left, b, a))
        blocks = [x[j : j + 8] for j in range(0, HALF, 8) for x in (low, high)]
        cells.append(jnp.concatenate(blocks, axis=0))
    rest = jnp.concatenate(cells, axis=1)
    high = rest.astype(BF16)
    low = (rest - high.astype(F32)).astype(BF16)
    pack([high, low], (even_ref[...], odd_ref[...]), store)


def return_kernel(arrived_ref, send_ref, out_ref):
    index = columns(send_ref[...].reshape(SLOTS, PEERS))
    out_ref[...] = unpack(
        lambda r: arrived_ref[pl.ds(r, PEERS, stride=ROWS), :],
        (one_hot(index, 0), one_hot(index, 1)),
        2,
    )


def vmem(x):
    return pltpu.with_memory_space_constraint(x, pltpu.VMEM)


def hbm(x):
    return pltpu.with_memory_space_constraint(x, pltpu.HBM)


def exchange(rows):
    blocks = rows.reshape(PEERS, ROWS, 128)
    moved = lax.all_to_all(blocks, ("circ", "span"), split_axis=0, concat_axis=0, tiled=True)
    return moved.reshape(PEERS * ROWS, 128)


def local(elem_rows, coupling, inverses, send_rows, recv_cells, slot_counts):
    send = jnp.transpose(send_rows, (2, 0, 1))
    cells = jnp.transpose(recv_cells, (2, 0, 1))
    packed_rows = (PEERS * ROWS, LANES)
    hot_shape = jax.ShapeDtypeStruct((PAIRS * PEERS, CELLS), BF16)
    bundle_shape = jax.ShapeDtypeStruct((SEGMENT, HALF, FEATURES, LANES), BF16)
    state_shape = jax.ShapeDtypeStruct((HALF, LANES), F32)
    forcing_shape = jax.ShapeDtypeStruct((SEGMENT, HALF, LANES), F32)
    in_hbm = pl.BlockSpec(memory_space=pltpu.HBM)
    outgoing = pl.pallas_call(
        pack_rows_kernel,
        out_shape=jax.ShapeDtypeStruct(packed_rows, BF16),
        in_specs=[in_hbm, IN_VMEM],
        out_specs=IN_VMEM,
        scratch_shapes=[
            pltpu.VMEM(packed_rows, F32),
            pltpu.VMEM(elem_rows.shape, BF16),
            pltpu.SemaphoreType.DMA,
        ],
        compiler_params=params(16),
        name="pack_rows",
    )(hbm(elem_rows), send)
    arrived = exchange(outgoing)
    bundles = pl.pallas_call(
        bundle_kernel,
        out_shape=[pltpu.HBM(bundle_shape.shape, BF16)] * 2,
        in_specs=[in_hbm],
        out_specs=[in_hbm] * 2,
        scratch_shapes=[
            pltpu.VMEM(coupling.shape, BF16),
            pltpu.VMEM(bundle_shape.shape, BF16),
            pltpu.VMEM(bundle_shape.shape, BF16),
            pltpu.SemaphoreType.DMA((3, SEGMENT)),
        ],
        compiler_params=params(32),
        cost_estimate=pl.CostEstimate(flops=0, bytes_accessed=4 * coupling.size, transcendentals=0),
        name="bundle",
    )(hbm(coupling))
    *forcings, even, odd, bundle_a, end_a = pl.pallas_call(
        forcing_kernel,
        out_shape=[forcing_shape] * 2 + [hot_shape] * 2 + [bundle_shape, state_shape],
        in_specs=[IN_VMEM] * 3 + [in_hbm] * 2,
        out_specs=[IN_VMEM] * 6,
        scratch_shapes=[
            pltpu.VMEM(packed_rows, F32),
            pltpu.VMEM((SEGMENT, FEATURES, LINES), F32),
            pltpu.VMEM(inverses.shape, BF16),
            pltpu.SemaphoreType.DMA((SEGMENT,)),
            pltpu.SemaphoreType.DMA((SEGMENT,)),
        ],
        compiler_params=params(24),
        name="forcing",
    )(arrived, cells, slot_counts, hbm(inverses), hbm(bundles[0]))
    even, odd = vmem(even), vmem(odd)
    forcings = [vmem(forcing) for forcing in forcings]
    end_b, bundle_b = pl.pallas_call(
        first_hop_kernel,
        out_shape=[state_shape, bundle_shape],
        in_specs=[in_hbm, IN_VMEM],
        out_specs=[IN_VMEM] * 2,
        scratch_shapes=[pltpu.SemaphoreType.DMA((SEGMENT,))],
        compiler_params=params(8),
        name="first_hop",
    )(hbm(bundles[1]), forcings[1])
    bundles = [
        vmem(
            pl.pallas_call(
                widen_kernel,
                out_shape=jax.ShapeDtypeStruct(bundle_shape.shape, F32),
                in_specs=[in_hbm, IN_VMEM],
                out_specs=IN_VMEM,
                scratch_shapes=[
                    pltpu.VMEM(bundle_shape.shape[1:], BF16),
                    pltpu.SemaphoreType.DMA,
                ],
                compiler_params=params(4),
                cost_estimate=pl.CostEstimate(
                    flops=2 * 10**6, bytes_accessed=2 * bundle_shape.size, transcendentals=0
                ),
                name="widen",
            )(hbm(source), vmem(near))
        )
        for source, near in zip(bundles, (bundle_a, bundle_b))
    ]

    def sweep(side, kernel, states, shape, name):
        operands = [*states, bundles[side], forcings[side]]
        return pl.pallas_call(
            kernel,
            out_shape=shape,
            in_specs=[IN_VMEM] * len(operands),
            out_specs=IN_VMEM,
            compiler_params=params(8),
            cost_estimate=pl.CostEstimate(
                flops=2 * 10**6, bytes_accessed=2 * bundle_shape.size, transcendentals=0
            ),
            name=name + "ab"[side],
        )(*operands)

    arrivals = ([], [])
    for hop in range(2 * N_CIRC - 1):
        for side in range(2):
            end = (end_a, end_b)[side]
            if hop:
                kernel = functools.partial(hop_kernel, hop)
                end = sweep(side, kernel, arrivals[side][-1:], state_shape, "hop_")
            pair = (hop % N_CIRC, (hop + 1) % N_CIRC)
            arrivals[side].append(lax.ppermute(end, "circ", [pair]))
    solved = [
        sweep(side, final_kernel, arrivals[side][N_CIRC - 1 :], forcing_shape, "final_")
        for side in range(2)
    ]

    returning = pl.pallas_call(
        return_pack_kernel,
        out_shape=jax.ShapeDtypeStruct(packed_rows, F32),
        in_specs=[IN_VMEM] * 4,
        out_specs=IN_VMEM,
        compiler_params=params(16),
        name="return_pack",
    )(*solved, even, odd)
    returned = exchange(returning)
    return pl.pallas_call(
        return_kernel,
        out_shape=jax.ShapeDtypeStruct((FEATURES, CELLS), F32),
        in_specs=[IN_VMEM] * 2,
        out_specs=IN_VMEM,
        compiler_params=params(16),
        name="return_rows",
    )(returned, send)


def solution(mesh):
    return jax.shard_map(
        local,
        mesh=mesh,
        in_specs=(
            P(None, ("circ", "span")),
            P("circ", None, None, "span"),
            P("circ", None, None, "span"),
            P(("circ", "span"), None, None),
            P(("circ", "span"), None, None),
            P(("circ", "span"), None),
        ),
        out_specs=P(None, ("circ", "span")),
        check_vma=False,
    )
```

```python
import functools

import jax
import jax.numpy as jnp
from jax import lax
from jax.experimental import pallas as pl
from jax.experimental.pallas import tpu as pltpu
from jax.sharding import PartitionSpec as P

FEATURES = 80
SEGMENT = 6
LINES = 128
CELLS = SEGMENT * LINES
PEERS = 128
SLOTS = 12
PAIRS = SLOTS // 2
ROWS = 8
MAIN = 64
TAIL = FEATURES - MAIN
N_CIRC = 8
NEAR = 2
HALF = FEATURES // 2
LANES = 128
SIDE = LANES // 2

IN_VMEM = pl.BlockSpec(memory_space=pltpu.VMEM)
F32 = jnp.float32
BF16 = jnp.bfloat16


def params(megabytes):
    return pltpu.CompilerParams(vmem_limit_bytes=megabytes * 2**20)


def fold_sublanes(parts, row):
    upper = row < 4
    fours = []
    for k in range(4):
        a, b = parts[k], parts[k + 4]
        fours.append(jnp.where(upper, a, b) + pltpu.roll(jnp.where(upper, b, a), 4, 0))
    even_pair = (row & 2) == 0
    twos = []
    for k in range(2):
        a, b = fours[k], fours[k + 2]
        twos.append(jnp.where(even_pair, a + pltpu.roll(a, 6, 0), b + pltpu.roll(b, 2, 0)))
    even = (row & 1) == 0
    a, b = twos
    return jnp.where(even, a + pltpu.roll(a, 7, 0), b + pltpu.roll(b, 1, 0))


def matvec(blocks_ref, position, vector, row):
    result = []
    for group in range(blocks_ref.shape[1] // 8):
        parts = []
        for k in range(8):
            terms = blocks_ref[position, group * 8 + k].astype(F32) * vector
            total = terms[0:8]
            for j in (*range(16, FEATURES, 16), *range(8, FEATURES, 16)):
                total = total + terms[j : j + 8]
            parts.append(total)
        result.append(fold_sublanes(parts, row))
    return jnp.concatenate(result, axis=0)


def sublane_ids():
    return lax.broadcasted_iota(jnp.int32, (8, LINES), 0)


def columns(table):
    padded = jnp.concatenate([table, jnp.full((16 - SLOTS, PEERS), -1, jnp.int32)], axis=0)
    return jnp.transpose(padded)


def one_hot(index, first):
    place = lax.broadcasted_iota(jnp.int32, (PEERS, CELLS), 1)
    return jnp.concatenate(
        [
            jnp.where(index[:, 2 * pair + first : 2 * pair + first + 1] == place, 1.0, 0.0).astype(BF16)
            for pair in range(PAIRS)
        ],
        axis=0,
    )


def across(a, b):
    return lax.dot_general(a, b, (((1,), (1,)), ((), ())), preferred_element_type=F32)


def down(a, b):
    return lax.dot_general(a, b, (((0,), (0,)), ((), ())), preferred_element_type=F32)


def spread(rows, offset):
    tail_at = 128 + (0 if offset == 0 else TAIL)
    parts = [rows[:MAIN], rows[MAIN:]]
    gaps = [offset, tail_at - offset - MAIN, 256 - tail_at - TAIL]
    filled = []
    for gap, part in zip(gaps, parts + [None]):
        if gap:
            filled.append(jnp.zeros((gap, CELLS), BF16))
        if part is not None:
            filled.append(part)
    return jnp.concatenate(filled, axis=0)


def swap(x):
    return pltpu.roll(x, SIDE, 1)


def left(rows):
    return lax.broadcasted_iota(jnp.int32, (rows, LANES), 1) < SIDE


def pack(pieces, hots, store):
    packed = 0.0
    for hot, offset in zip(hots, (0, MAIN)):
        for piece in pieces:
            packed = packed + across(hot, spread(piece, offset))
    tails = []
    for pair in range(PAIRS):
        rows = packed[pair * PEERS : (pair + 1) * PEERS]
        store(pair, rows[:, :128])
        tail = rows[:, 128:]
        shift = 2 * TAIL * (pair % 4)
        tails.append(pltpu.roll(tail, shift, 1) if shift else tail)
    store(6, tails[0] + tails[1] + tails[2] + tails[3])
    store(7, tails[4] + tails[5])


def unpack(load, hots, pieces):
    lane = lax.broadcasted_iota(jnp.int32, (PEERS, 128), 1)
    last = (load(6), load(7))
    total = 0.0
    for first in range(2):
        slots = []
        for pair in range(PAIRS):
            rows = load(pair)
            if first:
                rows = pltpu.roll(rows, MAIN, 1)
            shift = (MAIN - 2 * TAIL * (pair % 4) - TAIL * first) % 128
            tail = last[pair // 4]
            tail = pltpu.roll(tail, shift, 1) if shift else tail
            slots.append(jnp.where(lane < MAIN, rows, jnp.where(lane < FEATURES, tail, 0.0)))
        slots = jnp.concatenate(slots, axis=0)
        hot = hots[first]
        for _ in range(pieces):
            part = slots.astype(BF16)
            total = total + down(part, hot)
            slots = slots - part.astype(F32)
    return total[:FEATURES]


def pack_rows_kernel(rows_hbm, send_ref, out_ref, wide, rows_ref, sem):
    copy = pltpu.make_async_copy(rows_hbm, rows_ref, sem)
    copy.start()

    def store(r, block):
        wide[pl.ds(r, PEERS, stride=ROWS), :] = block

    index = columns(send_ref[...].reshape(SLOTS, PEERS))
    hots = one_hot(index, 0), one_hot(index, 1)
    copy.wait()
    pack([rows_ref[...]], hots, store)
    out_ref[...] = wide[...].astype(BF16)


def bundle_kernel(
    coupling_hbm, inverses_hbm, bundle_a_hbm, bundle_b_hbm, near_ref,
    whole, bundle_a, bundle_b, sems, near_sem,
):
    fetch, put_a, put_b = [
        [pltpu.make_async_copy(src.at[p], dst.at[p], sems.at[k, p]) for p in range(SEGMENT)]
        for k, (src, dst) in enumerate(
            ((coupling_hbm, whole), (bundle_a, bundle_a_hbm), (bundle_b, bundle_b_hbm))
        )
    ]
    for copy in fetch:
        copy.start()
    near = pltpu.make_async_copy(inverses_hbm.at[pl.ds(0, NEAR)], near_ref, near_sem)
    near.start()
    on_left = left(FEATURES)
    for p in range(SEGMENT):
        fetch[p].wait()

        @pl.loop(0, HALF // 8)
        def _(block):
            for k in range(8):
                low = whole[p, block * 16 + k]
                high = whole[p, block * 16 + 8 + k].astype(F32)
                high = jnp.concatenate(
                    [swap(high[j * 8 : j * 8 + 8]) for i in range(HALF // 8) for j in (2 * i + 1, 2 * i)],
                    axis=0,
                ).astype(BF16)
                bundle_a[p, block * 8 + k] = jnp.where(on_left, low, high)
                bundle_b[p, block * 8 + k] = jnp.where(on_left, high, low)

        put_a[p].start()
        put_b[p].start()
    for copy in put_a + put_b:
        copy.wait()
    near.wait()


def blocks8(x, odd):
    return jnp.concatenate([x[j * 8 : j * 8 + 8] for j in range(odd, FEATURES // 8, 2)], axis=0)


def advance(coupling_ref, forcing_ref, first, state, record=None):
    row = sublane_ids()

    def step(position, state):
        own = [state[j : j + 8] for j in range(0, HALF, 8)]
        both = jnp.concatenate([x for block in own for x in (block, swap(block))], axis=0)
        state = forcing_ref[position] + matvec(coupling_ref, position, both, row)
        if record is not None:
            record[position] = state
        return state

    if callable(first):

        def waited(position, state):
            first(position)
            return step(position, state)

        return lax.fori_loop(1, SEGMENT, waited, state)
    return lax.fori_loop(first, SEGMENT, step, state, unroll=True)


def forcing_kernel(
    arrived_ref, cells_ref, counts_ref, near_ref, inverses_hbm, bundle_hbm,
    forcing_a, forcing_b, bundle_ref, end_ref,
    wide, lines, inverses_ref, sems, bundle_sems,
):
    def copy(p):
        return pltpu.make_async_copy(inverses_hbm.at[p], inverses_ref.at[p], sems.at[p])

    def bundle_copy(p):
        return pltpu.make_async_copy(bundle_hbm.at[p], bundle_ref.at[p], bundle_sems.at[p])

    for p in range(NEAR, SEGMENT):
        copy(p).start()
    wide[...] = arrived_ref[...].astype(F32)
    slot = lax.broadcasted_iota(jnp.int32, (SLOTS, PEERS), 0)
    index = columns(jnp.where(slot < counts_ref[...], cells_ref[...].reshape(SLOTS, PEERS), -1))
    hots = one_hot(index, 0), one_hot(index, 1)
    found = unpack(lambda r: wide[pl.ds(r, PEERS, stride=ROWS), :], hots, 1)
    for p in range(SEGMENT):
        lines[p] = found[:, p * LINES : (p + 1) * LINES]
    row = sublane_ids()
    on_left = left(HALF)

    def force(p, blocks_ref):
        forcing = matvec(blocks_ref, p, lines[p], row)
        low, high = blocks8(forcing, 0), swap(blocks8(forcing, 1))
        forcing_a[p] = jnp.where(on_left, low, high)
        forcing_b[p] = jnp.where(on_left, high, low)

    @pl.loop(0, NEAR)
    def _(p):
        bundle_copy(p + 1).start()
        force(p, near_ref)

    @pl.loop(NEAR, SEGMENT)
    def _(p):
        copy(p).wait()

        @pl.when(p + 1 < SEGMENT)
        def _():
            bundle_copy(p + 1).start()

        force(p, inverses_ref)

    end_ref[...] = advance(
        bundle_ref, forcing_a, lambda p: bundle_copy(p).wait(), forcing_a[0]
    )


def hots_kernel(cells_ref, counts_ref, even_ref, odd_ref):
    slot = lax.broadcasted_iota(jnp.int32, (SLOTS, PEERS), 0)
    index = columns(jnp.where(slot < counts_ref[...], cells_ref[...].reshape(SLOTS, PEERS), -1))
    even_ref[...] = one_hot(index, 0)
    odd_ref[...] = one_hot(index, 1)


def here(hop):
    return lax.axis_index("circ") == hop % N_CIRC


def first_hop_kernel(bundle_hbm, forcing_ref, end_ref, bundle_ref, sems):
    def copy(p):
        return pltpu.make_async_copy(bundle_hbm.at[p], bundle_ref.at[p], sems.at[p])

    for p in range(1, SEGMENT):
        copy(p).start()
    end_ref[...] = advance(bundle_ref, forcing_ref, lambda p: copy(p).wait(), forcing_ref[0])


def widen_kernel(bundle_hbm, bundle_ref, wide_ref, first, sem):
    copy = pltpu.make_async_copy(bundle_hbm.at[0], first, sem)
    copy.start()

    @pl.loop(1, SEGMENT)
    def _(p):
        @pl.loop(0, HALF, unroll=8)
        def _(i):
            wide_ref[p, i] = bundle_ref[p, i].astype(F32)

    copy.wait()

    @pl.loop(0, HALF, unroll=8)
    def _(i):
        wide_ref[0, i] = first[i].astype(F32)


def hop_kernel(hop, state_ref, coupling_ref, forcing_ref, end_ref):
    @pl.when(here(hop))
    def _():
        end_ref[...] = advance(coupling_ref, forcing_ref, 0, state_ref[...])


def final_kernel(*refs):
    *state_refs, coupling_ref, forcing_ref, solved_ref = refs
    state = state_refs[0][...]
    for ref in state_refs[1:]:
        state = state + ref[...]
    advance(coupling_ref, forcing_ref, 0, state, solved_ref)


def return_pack_kernel(solved_a, solved_b, even_ref, odd_ref, out_ref):
    def store(r, block):
        out_ref[pl.ds(r, PEERS, stride=ROWS), :] = block

    on_left = left(HALF)
    cells = []
    for position in range(SEGMENT):
        a, b = solved_a[position], solved_b[position]
        low = jnp.where(on_left, a, b)
        high = swap(jnp.where(on_left, b, a))
        blocks = [x[j : j + 8] for j in range(0, HALF, 8) for x in (low, high)]
        cells.append(jnp.concatenate(blocks, axis=0))
    rest = jnp.concatenate(cells, axis=1)
    high = rest.astype(BF16)
    low = (rest - high.astype(F32)).astype(BF16)
    pack([high, low], (even_ref[...], odd_ref[...]), store)


def return_kernel(arrived_ref, send_ref, out_ref):
    index = columns(send_ref[...].reshape(SLOTS, PEERS))
    out_ref[...] = unpack(
        lambda r: arrived_ref[pl.ds(r, PEERS, stride=ROWS), :],
        (one_hot(index, 0), one_hot(index, 1)),
        2,
    )


def vmem(x):
    return pltpu.with_memory_space_constraint(x, pltpu.VMEM)


def hbm(x):
    return pltpu.with_memory_space_constraint(x, pltpu.HBM)


def exchange(rows):
    blocks = rows.reshape(PEERS, ROWS, 128)
    moved = lax.all_to_all(blocks, ("circ", "span"), split_axis=0, concat_axis=0, tiled=True)
    return moved.reshape(PEERS * ROWS, 128)


def local(elem_rows, coupling, inverses, send_rows, recv_cells, slot_counts):
    send = jnp.transpose(send_rows, (2, 0, 1))
    cells = jnp.transpose(recv_cells, (2, 0, 1))
    packed_rows = (PEERS * ROWS, LANES)
    hot_shape = jax.ShapeDtypeStruct((PAIRS * PEERS, CELLS), BF16)
    bundle_shape = jax.ShapeDtypeStruct((SEGMENT, HALF, FEATURES, LANES), BF16)
    state_shape = jax.ShapeDtypeStruct((HALF, LANES), F32)
    forcing_shape = jax.ShapeDtypeStruct((SEGMENT, HALF, LANES), F32)
    in_hbm = pl.BlockSpec(memory_space=pltpu.HBM)
    outgoing = pl.pallas_call(
        pack_rows_kernel,
        out_shape=jax.ShapeDtypeStruct(packed_rows, BF16),
        in_specs=[in_hbm, IN_VMEM],
        out_specs=IN_VMEM,
        scratch_shapes=[
            pltpu.VMEM(packed_rows, F32),
            pltpu.VMEM(elem_rows.shape, BF16),
            pltpu.SemaphoreType.DMA,
        ],
        compiler_params=params(16),
        name="pack_rows",
    )(hbm(elem_rows), send)
    arrived = exchange(outgoing)
    *bundles, near = pl.pallas_call(
        bundle_kernel,
        out_shape=[pltpu.HBM(bundle_shape.shape, BF16)] * 2
        + [jax.ShapeDtypeStruct((NEAR, *inverses.shape[1:]), BF16)],
        in_specs=[in_hbm] * 2,
        out_specs=[in_hbm] * 2 + [IN_VMEM],
        scratch_shapes=[
            pltpu.VMEM(coupling.shape, BF16),
            pltpu.VMEM(bundle_shape.shape, BF16),
            pltpu.VMEM(bundle_shape.shape, BF16),
            pltpu.SemaphoreType.DMA((3, SEGMENT)),
            pltpu.SemaphoreType.DMA,
        ],
        compiler_params=params(32),
        cost_estimate=pl.CostEstimate(flops=0, bytes_accessed=4 * coupling.size, transcendentals=0),
        name="bundle",
    )(hbm(coupling), hbm(inverses))
    *forcings, bundle_a, end_a = pl.pallas_call(
        forcing_kernel,
        out_shape=[forcing_shape] * 2 + [bundle_shape, state_shape],
        in_specs=[IN_VMEM] * 4 + [in_hbm] * 2,
        out_specs=[IN_VMEM] * 4,
        scratch_shapes=[
            pltpu.VMEM(packed_rows, F32),
            pltpu.VMEM((SEGMENT, FEATURES, LINES), F32),
            pltpu.VMEM(inverses.shape, BF16),
            pltpu.SemaphoreType.DMA((SEGMENT,)),
            pltpu.SemaphoreType.DMA((SEGMENT,)),
        ],
        compiler_params=params(24),
        name="forcing",
    )(arrived, cells, slot_counts, vmem(near), hbm(inverses), hbm(bundles[0]))
    forcings = [vmem(forcing) for forcing in forcings]
    end_b, bundle_b = pl.pallas_call(
        first_hop_kernel,
        out_shape=[state_shape, bundle_shape],
        in_specs=[in_hbm, IN_VMEM],
        out_specs=[IN_VMEM] * 2,
        scratch_shapes=[pltpu.SemaphoreType.DMA((SEGMENT,))],
        compiler_params=params(8),
        name="first_hop",
    )(hbm(bundles[1]), forcings[1])
    bundles = [
        vmem(
            pl.pallas_call(
                widen_kernel,
                out_shape=jax.ShapeDtypeStruct(bundle_shape.shape, F32),
                in_specs=[in_hbm, IN_VMEM],
                out_specs=IN_VMEM,
                scratch_shapes=[
                    pltpu.VMEM(bundle_shape.shape[1:], BF16),
                    pltpu.SemaphoreType.DMA,
                ],
                compiler_params=params(4),
                cost_estimate=pl.CostEstimate(
                    flops=2 * 10**6, bytes_accessed=2 * bundle_shape.size, transcendentals=0
                ),
                name="widen",
            )(hbm(source), vmem(near))
        )
        for source, near in zip(bundles, (bundle_a, bundle_b))
    ]

    def sweep(side, kernel, states, shape, name):
        operands = [*states, bundles[side], forcings[side]]
        return pl.pallas_call(
            kernel,
            out_shape=shape,
            in_specs=[IN_VMEM] * len(operands),
            out_specs=IN_VMEM,
            compiler_params=params(8),
            cost_estimate=pl.CostEstimate(
                flops=2 * 10**6, bytes_accessed=2 * bundle_shape.size, transcendentals=0
            ),
            name=name + "ab"[side],
        )(*operands)

    cells, counts, _ = lax.optimization_barrier((cells, slot_counts, end_b))
    even, odd = pl.pallas_call(
        hots_kernel,
        out_shape=[hot_shape] * 2,
        in_specs=[IN_VMEM] * 2,
        out_specs=[IN_VMEM] * 2,
        compiler_params=params(8),
        name="hots",
    )(cells, counts)
    arrivals = ([], [])
    for hop in range(2 * N_CIRC - 1):
        for side in range(2):
            end = (end_a, end_b)[side]
            if hop:
                kernel = functools.partial(hop_kernel, hop)
                end = sweep(side, kernel, arrivals[side][-1:], state_shape, "hop_")
            pair = (hop % N_CIRC, (hop + 1) % N_CIRC)
            arrivals[side].append(lax.ppermute(end, "circ", [pair]))
    solved = [
        sweep(side, final_kernel, arrivals[side][N_CIRC - 1 :], forcing_shape, "final_")
        for side in range(2)
    ]

    returning = pl.pallas_call(
        return_pack_kernel,
        out_shape=jax.ShapeDtypeStruct(packed_rows, F32),
        in_specs=[IN_VMEM] * 4,
        out_specs=IN_VMEM,
        compiler_params=params(16),
        name="return_pack",
    )(*solved, vmem(even), vmem(odd))
    returned = exchange(returning)
    return pl.pallas_call(
        return_kernel,
        out_shape=jax.ShapeDtypeStruct((FEATURES, CELLS), F32),
        in_specs=[IN_VMEM] * 2,
        out_specs=IN_VMEM,
        compiler_params=params(16),
        name="return_rows",
    )(returned, send)


def solution(mesh):
    return jax.shard_map(
        local,
        mesh=mesh,
        in_specs=(
            P(None, ("circ", "span")),
            P("circ", None, None, "span"),
            P("circ", None, None, "span"),
            P(("circ", "span"), None, None),
            P(("circ", "span"), None, None),
            P(("circ", "span"), None),
        ),
        out_specs=P(None, ("circ", "span")),
        check_vma=False,
    )
```

```python
import functools

import jax
import jax.numpy as jnp
from jax import lax
from jax.experimental import pallas as pl
from jax.experimental.pallas import tpu as pltpu
from jax.sharding import PartitionSpec as P

FEATURES = 80
SEGMENT = 6
LINES = 128
CELLS = SEGMENT * LINES
PEERS = 128
SLOTS = 12
PAIRS = SLOTS // 2
ROWS = 8
MAIN = 64
TAIL = FEATURES - MAIN
N_CIRC = 8
STEPS = 32000.0
SMALLEST = 2.0**-100
NEAR = 2
HALF = FEATURES // 2
LANES = 128
SIDE = LANES // 2

IN_VMEM = pl.BlockSpec(memory_space=pltpu.VMEM)
F32 = jnp.float32
BF16 = jnp.bfloat16


def params(megabytes):
    return pltpu.CompilerParams(vmem_limit_bytes=megabytes * 2**20)


def fold_sublanes(parts, row):
    upper = row < 4
    fours = []
    for k in range(4):
        a, b = parts[k], parts[k + 4]
        fours.append(jnp.where(upper, a, b) + pltpu.roll(jnp.where(upper, b, a), 4, 0))
    even_pair = (row & 2) == 0
    twos = []
    for k in range(2):
        a, b = fours[k], fours[k + 2]
        twos.append(jnp.where(even_pair, a + pltpu.roll(a, 6, 0), b + pltpu.roll(b, 2, 0)))
    even = (row & 1) == 0
    a, b = twos
    return jnp.where(even, a + pltpu.roll(a, 7, 0), b + pltpu.roll(b, 1, 0))


def matvec(blocks_ref, position, vector, row):
    result = []
    for group in range(blocks_ref.shape[1] // 8):
        parts = []
        for k in range(8):
            terms = blocks_ref[position, group * 8 + k].astype(F32) * vector
            total = terms[0:8]
            for j in (*range(16, FEATURES, 16), *range(8, FEATURES, 16)):
                total = total + terms[j : j + 8]
            parts.append(total)
        result.append(fold_sublanes(parts, row))
    return jnp.concatenate(result, axis=0)


def sublane_ids():
    return lax.broadcasted_iota(jnp.int32, (8, LINES), 0)


def columns(table):
    padded = jnp.concatenate([table, jnp.full((16 - SLOTS, PEERS), -1, jnp.int32)], axis=0)
    return jnp.transpose(padded)


def one_hot(index, first):
    place = lax.broadcasted_iota(jnp.int32, (PEERS, CELLS), 1)
    return jnp.concatenate(
        [
            jnp.where(index[:, 2 * pair + first : 2 * pair + first + 1] == place, 1.0, 0.0).astype(BF16)
            for pair in range(PAIRS)
        ],
        axis=0,
    )


def across(a, b):
    return lax.dot_general(a, b, (((1,), (1,)), ((), ())), preferred_element_type=F32)


def down(a, b):
    return lax.dot_general(a, b, (((0,), (0,)), ((), ())), preferred_element_type=F32)


def swap(x):
    return pltpu.roll(x, SIDE, 1)


def left(rows):
    return lax.broadcasted_iota(jnp.int32, (rows, LANES), 1) < SIDE


def spread(rows, odd, extra):
    parts = [jnp.zeros((MAIN, CELLS), BF16), jnp.zeros((TAIL, CELLS), BF16)]
    at = slice(None, None, -1) if odd else slice(None)
    main = [rows[:MAIN], parts[0]][at]
    tail = [rows[MAIN:], parts[1]][at]
    if extra is None:
        note = parts[1]
    else:
        place = lax.broadcasted_iota(jnp.int32, (TAIL, CELLS), 0)
        note = jnp.where(place == odd, extra, 0.0).astype(BF16)
    rest = jnp.zeros((128 - 3 * TAIL, CELLS), BF16)
    return jnp.concatenate([*main, *tail, note, rest], axis=0)


def pack(pieces, hots, store, extra=None):
    packed = 0.0
    for odd, hot in enumerate(hots):
        for k, piece in enumerate(pieces):
            packed = packed + across(hot, spread(piece, odd, None if k else extra))
    lane = lax.broadcasted_iota(jnp.int32, (PEERS, LANES), 1)
    tails = []
    notes = 0.0
    for pair in range(PAIRS):
        rows = packed[pair * PEERS : (pair + 1) * PEERS]
        store(pair, rows[:, :128])
        tail = rows[:, 128:]
        if extra is not None:
            notes = notes + pltpu.roll(jnp.where(lane < 2 * TAIL, 0.0, tail), 2 * TAIL + 2 * pair, 1)
            tail = jnp.where(lane < 2 * TAIL, tail, 0.0)
        shift = 2 * TAIL * (pair % 4)
        tails.append(pltpu.roll(tail, shift, 1) if shift else tail)
    store(6, tails[0] + tails[1] + tails[2] + tails[3])
    store(7, tails[4] + tails[5] + notes)


def unpack(load, hots, pieces, noted=False):
    lane = lax.broadcasted_iota(jnp.int32, (PEERS, LANES), 1)
    last = (load(6), load(7))
    total = 0.0
    for odd in range(2):
        slots = []
        for pair in range(PAIRS):
            rows = load(pair)
            if odd:
                rows = pltpu.roll(rows, MAIN, 1)
            shift = (MAIN - 2 * TAIL * (pair % 4) - TAIL * odd) % LANES
            tail = last[pair // 4]
            tail = pltpu.roll(tail, shift, 1) if shift else tail
            note = 0.0
            if noted:
                note = pltpu.roll(last[1], FEATURES - MAIN - 2 * pair - odd, 1)
                note = jnp.where(lane == FEATURES, note, 0.0)
            slots.append(jnp.where(lane < MAIN, rows, jnp.where(lane < FEATURES, tail, note)))
        slots = jnp.concatenate(slots, axis=0)
        hot = hots[odd]
        for _ in range(pieces):
            part = slots.astype(BF16)
            total = total + down(part, hot)
            slots = slots - part.astype(F32)
    if noted:
        return total[:FEATURES], total[FEATURES : FEATURES + 8]
    return total[:FEATURES]


def pack_rows_kernel(rows_hbm, send_ref, out_ref, wide, rows_ref, sem):
    copy = pltpu.make_async_copy(rows_hbm, rows_ref, sem)
    copy.start()

    def store(r, block):
        wide[pl.ds(r, PEERS, stride=ROWS), :] = block

    index = columns(send_ref[...].reshape(SLOTS, PEERS))
    hots = one_hot(index, 0), one_hot(index, 1)
    copy.wait()
    pack([rows_ref[...]], hots, store)
    out_ref[...] = wide[...].astype(BF16)


def bundle_kernel(
    coupling_hbm, inverses_hbm, bundle_a_hbm, bundle_b_hbm, near_ref,
    whole, bundle_a, bundle_b, sems, near_sem,
):
    fetch, put_a, put_b = [
        [pltpu.make_async_copy(src.at[p], dst.at[p], sems.at[k, p]) for p in range(SEGMENT)]
        for k, (src, dst) in enumerate(
            ((coupling_hbm, whole), (bundle_a, bundle_a_hbm), (bundle_b, bundle_b_hbm))
        )
    ]
    for copy in fetch:
        copy.start()
    near = pltpu.make_async_copy(inverses_hbm.at[pl.ds(0, NEAR)], near_ref, near_sem)
    near.start()
    on_left = left(FEATURES)
    for p in range(SEGMENT):
        fetch[p].wait()

        @pl.loop(0, HALF // 8)
        def _(block):
            for k in range(8):
                low = whole[p, block * 16 + k]
                high = whole[p, block * 16 + 8 + k].astype(F32)
                high = jnp.concatenate(
                    [swap(high[j * 8 : j * 8 + 8]) for i in range(HALF // 8) for j in (2 * i + 1, 2 * i)],
                    axis=0,
                ).astype(BF16)
                bundle_a[p, block * 8 + k] = jnp.where(on_left, low, high)
                bundle_b[p, block * 8 + k] = jnp.where(on_left, high, low)

        put_a[p].start()
        put_b[p].start()
    for copy in put_a + put_b:
        copy.wait()
    near.wait()


def blocks8(x, odd):
    return jnp.concatenate([x[j * 8 : j * 8 + 8] for j in range(odd, FEATURES // 8, 2)], axis=0)


def move(coupling_ref, at, forcing, state):
    own = [state[j : j + 8] for j in range(0, HALF, 8)]
    both = jnp.concatenate([x for block in own for x in (block, swap(block))], axis=0)
    return forcing + matvec(coupling_ref, at, both, sublane_ids())


def advance(coupling_ref, forcing_ref, first, state, record=None):
    def step(position, state):
        if callable(first):
            first(position)
        state = move(coupling_ref, position, forcing_ref[position], state)
        if record is not None:
            record[position] = state
        return state

    if callable(first):
        return lax.fori_loop(1, SEGMENT, step, state)
    return lax.fori_loop(first, SEGMENT, step, state, unroll=True)


def forcing_kernel(
    arrived_ref, cells_ref, counts_ref, near_ref, inverses_hbm, bundle_hbm,
    forcing_a, forcing_b, bundle_ref, end_ref,
    wide, lines, inverses_ref, sems, bundle_sems,
):
    def copy(p):
        return pltpu.make_async_copy(inverses_hbm.at[p], inverses_ref.at[p], sems.at[p])

    def bundle_copy(p):
        return pltpu.make_async_copy(bundle_hbm.at[p], bundle_ref.at[p], bundle_sems.at[p])

    for p in range(NEAR, SEGMENT):
        copy(p).start()
    wide[...] = arrived_ref[...].astype(F32)
    slot = lax.broadcasted_iota(jnp.int32, (SLOTS, PEERS), 0)
    index = columns(jnp.where(slot < counts_ref[...], cells_ref[...].reshape(SLOTS, PEERS), -1))
    hots = one_hot(index, 0), one_hot(index, 1)
    found = unpack(lambda r: wide[pl.ds(r, PEERS, stride=ROWS), :], hots, 1)
    for p in range(SEGMENT):
        lines[p] = found[:, p * LINES : (p + 1) * LINES]
    row = sublane_ids()
    on_left = left(HALF)

    def force(p, blocks_ref):
        forcing = matvec(blocks_ref, p, lines[p], row)
        low, high = blocks8(forcing, 0), swap(blocks8(forcing, 1))
        forcing_a[p] = jnp.where(on_left, low, high)
        forcing_b[p] = jnp.where(on_left, high, low)

    @pl.loop(0, NEAR)
    def _(p):
        bundle_copy(p + 1).start()
        force(p, near_ref)

    @pl.loop(NEAR, SEGMENT)
    def _(p):
        copy(p).wait()

        @pl.when(p + 1 < SEGMENT)
        def _():
            bundle_copy(p + 1).start()

        force(p, inverses_ref)

    end_ref[...] = advance(
        bundle_ref, forcing_a, lambda p: bundle_copy(p).wait(), forcing_a[0]
    )


def hots_kernel(cells_ref, counts_ref, even_ref, odd_ref):
    slot = lax.broadcasted_iota(jnp.int32, (SLOTS, PEERS), 0)
    index = columns(jnp.where(slot < counts_ref[...], cells_ref[...].reshape(SLOTS, PEERS), -1))
    even_ref[...] = one_hot(index, 0)
    odd_ref[...] = one_hot(index, 1)


def here(hop):
    return lax.axis_index("circ") == hop % N_CIRC


def first_hop_kernel(
    bundle_a_hbm, bundle_b_hbm, forcing_ref, end_ref, head_ref, bundle_ref, sems, head_sem
):
    def copy(p):
        return pltpu.make_async_copy(bundle_b_hbm.at[p], bundle_ref.at[p], sems.at[p])

    for p in (*range(1, SEGMENT), 0):
        copy(p).start()
    head = pltpu.make_async_copy(bundle_a_hbm.at[pl.ds(0, 1)], head_ref, head_sem)
    head.start()
    end_ref[...] = advance(bundle_ref, forcing_ref, lambda p: copy(p).wait(), forcing_ref[0])
    copy(0).wait()
    head.wait()


def widen_kernel(after_ref, *refs):
    *heads, bundle_ref, wide_ref = refs

    def widen(p, from_ref, at):
        @pl.loop(0, HALF, unroll=8)
        def _(i):
            wide_ref[p, i] = from_ref[at, i].astype(F32)

    if heads:
        widen(0, heads[0], 0)

    @pl.loop(len(heads), SEGMENT)
    def _(p):
        widen(p, bundle_ref, p)


def second_hop_kernel(state_ref, head_ref, coupling_ref, forcing_ref, end_ref):
    @pl.when(here(1))
    def _():
        state = move(head_ref, 0, forcing_ref[0], state_ref[...])
        end_ref[...] = advance(coupling_ref, forcing_ref, 1, state)


def hop_kernel(hop, state_ref, coupling_ref, forcing_ref, end_ref):
    @pl.when(here(hop))
    def _():
        end_ref[...] = advance(coupling_ref, forcing_ref, 0, state_ref[...])


def final_kernel(*refs):
    *state_refs, coupling_ref, forcing_ref, solved_ref = refs
    state = state_refs[0][...]
    for ref in state_refs[1:]:
        state = state + ref[...]
    advance(coupling_ref, forcing_ref, 0, state, solved_ref)


def half_power(exponent):
    return jnp.exp2(0.5 * exponent)


def return_pack_kernel(solved_a, solved_b, even_ref, odd_ref, out_ref, wide):
    def store(r, block):
        wide[pl.ds(r, PEERS, stride=ROWS), :] = block

    on_left = left(HALF)
    cells = []
    for position in range(SEGMENT):
        a, b = solved_a[position], solved_b[position]
        low = jnp.where(on_left, a, b)
        high = swap(jnp.where(on_left, b, a))
        blocks = [x[j : j + 8] for j in range(0, HALF, 8) for x in (low, high)]
        cells.append(jnp.concatenate(blocks, axis=0))
    rest = jnp.concatenate(cells, axis=1)
    largest = jnp.max(jnp.abs(rest), axis=0, keepdims=True)
    exponent = jnp.ceil(jnp.log2(jnp.maximum(largest, SMALLEST)))
    shrink = half_power(-exponent)
    whole = jnp.floor(rest * shrink * shrink * STEPS + 0.5)
    high = whole.astype(BF16)
    low = (whole - high.astype(F32)).astype(BF16)
    pack([high, low], (even_ref[...], odd_ref[...]), store, exponent)
    out_ref[...] = wide[...].astype(jnp.int32).astype(jnp.int16)


def return_kernel(arrived_ref, send_ref, out_ref, wide):
    wide[...] = arrived_ref[...].astype(jnp.int32).astype(F32)
    index = columns(send_ref[...].reshape(SLOTS, PEERS))
    whole, exponent = unpack(
        lambda r: wide[pl.ds(r, PEERS, stride=ROWS), :],
        (one_hot(index, 0), one_hot(index, 1)),
        2,
        True,
    )
    grow = half_power(exponent[:1])
    out_ref[...] = whole * (1.0 / STEPS) * grow * grow


def vmem(x):
    return pltpu.with_memory_space_constraint(x, pltpu.VMEM)


def hbm(x):
    return pltpu.with_memory_space_constraint(x, pltpu.HBM)


def exchange(rows):
    blocks = rows.reshape(PEERS, ROWS, 128)
    moved = lax.all_to_all(blocks, ("circ", "span"), split_axis=0, concat_axis=0, tiled=True)
    return moved.reshape(PEERS * ROWS, 128)


def local(elem_rows, coupling, inverses, send_rows, recv_cells, slot_counts):
    send = jnp.transpose(send_rows, (2, 0, 1))
    cells = jnp.transpose(recv_cells, (2, 0, 1))
    packed_rows = (PEERS * ROWS, LANES)
    hot_shape = jax.ShapeDtypeStruct((PAIRS * PEERS, CELLS), BF16)
    bundle_shape = jax.ShapeDtypeStruct((SEGMENT, HALF, FEATURES, LANES), BF16)
    state_shape = jax.ShapeDtypeStruct((HALF, LANES), F32)
    forcing_shape = jax.ShapeDtypeStruct((SEGMENT, HALF, LANES), F32)
    in_hbm = pl.BlockSpec(memory_space=pltpu.HBM)
    outgoing = pl.pallas_call(
        pack_rows_kernel,
        out_shape=jax.ShapeDtypeStruct(packed_rows, BF16),
        in_specs=[in_hbm, IN_VMEM],
        out_specs=IN_VMEM,
        scratch_shapes=[
            pltpu.VMEM(packed_rows, F32),
            pltpu.VMEM(elem_rows.shape, BF16),
            pltpu.SemaphoreType.DMA,
        ],
        compiler_params=params(16),
        name="pack_rows",
    )(hbm(elem_rows), send)
    arrived = exchange(outgoing)
    *bundles, near = pl.pallas_call(
        bundle_kernel,
        out_shape=[pltpu.HBM(bundle_shape.shape, BF16)] * 2
        + [jax.ShapeDtypeStruct((NEAR, *inverses.shape[1:]), BF16)],
        in_specs=[in_hbm] * 2,
        out_specs=[in_hbm] * 2 + [IN_VMEM],
        scratch_shapes=[
            pltpu.VMEM(coupling.shape, BF16),
            pltpu.VMEM(bundle_shape.shape, BF16),
            pltpu.VMEM(bundle_shape.shape, BF16),
            pltpu.SemaphoreType.DMA((3, SEGMENT)),
            pltpu.SemaphoreType.DMA,
        ],
        compiler_params=params(32),
        cost_estimate=pl.CostEstimate(flops=0, bytes_accessed=4 * coupling.size, transcendentals=0),
        name="bundle",
    )(hbm(coupling), hbm(inverses))
    *forcings, bundle_a, end_a = pl.pallas_call(
        forcing_kernel,
        out_shape=[forcing_shape] * 2 + [bundle_shape, state_shape],
        in_specs=[IN_VMEM] * 4 + [in_hbm] * 2,
        out_specs=[IN_VMEM] * 4,
        scratch_shapes=[
            pltpu.VMEM(packed_rows, F32),
            pltpu.VMEM((SEGMENT, FEATURES, LINES), F32),
            pltpu.VMEM(inverses.shape, BF16),
            pltpu.SemaphoreType.DMA((SEGMENT,)),
            pltpu.SemaphoreType.DMA((SEGMENT,)),
        ],
        compiler_params=params(24),
        name="forcing",
    )(arrived, cells, slot_counts, vmem(near), hbm(inverses), hbm(bundles[0]))
    forcings = [vmem(forcing) for forcing in forcings]
    end_b, head_a, bundle_b = pl.pallas_call(
        first_hop_kernel,
        out_shape=[
            state_shape,
            jax.ShapeDtypeStruct((1, *bundle_shape.shape[1:]), BF16),
            bundle_shape,
        ],
        in_specs=[in_hbm, in_hbm, IN_VMEM],
        out_specs=[IN_VMEM] * 3,
        scratch_shapes=[pltpu.SemaphoreType.DMA((SEGMENT,)), pltpu.SemaphoreType.DMA],
        compiler_params=params(8),
        name="first_hop",
    )(hbm(bundles[0]), hbm(bundles[1]), forcings[1])
    narrow = [[vmem(head_a), vmem(bundle_a)], [vmem(bundle_b)]]
    sweep_cost = pl.CostEstimate(
        flops=2 * 10**6, bytes_accessed=2 * bundle_shape.size, transcendentals=0
    )

    def sweep(kernel, states, blocks, forcing, shape, name):
        operands = [*states, *blocks, forcing]
        return pl.pallas_call(
            kernel,
            out_shape=shape,
            in_specs=[IN_VMEM] * len(operands),
            out_specs=IN_VMEM,
            compiler_params=params(8),
            cost_estimate=sweep_cost,
            name=name,
        )(*operands)

    def widen(after, blocks):
        return vmem(
            pl.pallas_call(
                widen_kernel,
                out_shape=jax.ShapeDtypeStruct(bundle_shape.shape, F32),
                in_specs=[IN_VMEM] * (1 + len(blocks)),
                out_specs=IN_VMEM,
                compiler_params=params(4),
                cost_estimate=sweep_cost,
                name="widen",
            )(after, *blocks)
        )

    cells, counts, _ = lax.optimization_barrier((cells, slot_counts, end_b))
    even, odd = pl.pallas_call(
        hots_kernel,
        out_shape=[hot_shape] * 2,
        in_specs=[IN_VMEM] * 2,
        out_specs=[IN_VMEM] * 2,
        compiler_params=params(8),
        name="hots",
    )(cells, counts)
    arrivals = ([], [])
    blocks = narrow
    for hop in range(2 * N_CIRC - 1):
        pair = (hop % N_CIRC, (hop + 1) % N_CIRC)
        for side in range(2):
            end = (end_a, end_b)[side]
            if hop:
                kernel = functools.partial(hop_kernel, hop)
                if hop == 1 and side == 0:
                    kernel = second_hop_kernel
                end = sweep(
                    kernel, arrivals[side][-1:], blocks[side], forcings[side], state_shape, "hop_" + "ab"[side]
                )
            arrivals[side].append(lax.ppermute(end, "circ", [pair]))
        if hop == 1:
            blocks = [[widen(end, part)] for part in narrow]
    solved = [
        sweep(
            final_kernel, arrivals[side][N_CIRC - 1 :], blocks[side], forcings[side], forcing_shape, "final_" + "ab"[side]
        )
        for side in range(2)
    ]

    returning = pl.pallas_call(
        return_pack_kernel,
        out_shape=jax.ShapeDtypeStruct(packed_rows, jnp.int16),
        in_specs=[IN_VMEM] * 4,
        out_specs=IN_VMEM,
        scratch_shapes=[pltpu.VMEM(packed_rows, F32)],
        compiler_params=params(16),
        name="return_pack",
    )(*solved, vmem(even), vmem(odd))
    returned = exchange(returning)
    return pl.pallas_call(
        return_kernel,
        out_shape=jax.ShapeDtypeStruct((FEATURES, CELLS), F32),
        in_specs=[IN_VMEM] * 2,
        out_specs=IN_VMEM,
        scratch_shapes=[pltpu.VMEM(packed_rows, F32)],
        compiler_params=params(16),
        name="return_rows",
    )(returned, send)


def solution(mesh):
    return jax.shard_map(
        local,
        mesh=mesh,
        in_specs=(
            P(None, ("circ", "span")),
            P("circ", None, None, "span"),
            P("circ", None, None, "span"),
            P(("circ", "span"), None, None),
            P(("circ", "span"), None, None),
            P(("circ", "span"), None),
        ),
        out_specs=P(None, ("circ", "span")),
        check_vma=False,
    )
```

```python
import functools

import jax
import jax.numpy as jnp
from jax import lax
from jax.experimental import pallas as pl
from jax.experimental.pallas import tpu as pltpu
from jax.sharding import PartitionSpec as P

FEATURES = 80
SEGMENT = 6
LINES = 128
CELLS = SEGMENT * LINES
PEERS = 128
SLOTS = 12
PAIRS = SLOTS // 2
ROWS = 8
MAIN = 64
TAIL = FEATURES - MAIN
N_CIRC = 8
STEPS = 32000.0
SMALLEST = 2.0**-100
NEAR = 2
HALF = FEATURES // 2
LANES = 128
SIDE = LANES // 2

IN_VMEM = pl.BlockSpec(memory_space=pltpu.VMEM)
F32 = jnp.float32
BF16 = jnp.bfloat16


def params(megabytes):
    return pltpu.CompilerParams(vmem_limit_bytes=megabytes * 2**20)


def fold_sublanes(parts, row):
    upper = row < 4
    fours = []
    for k in range(4):
        a, b = parts[k], parts[k + 4]
        fours.append(jnp.where(upper, a, b) + pltpu.roll(jnp.where(upper, b, a), 4, 0))
    even_pair = (row & 2) == 0
    twos = []
    for k in range(2):
        a, b = fours[k], fours[k + 2]
        twos.append(jnp.where(even_pair, a + pltpu.roll(a, 6, 0), b + pltpu.roll(b, 2, 0)))
    even = (row & 1) == 0
    a, b = twos
    return jnp.where(even, a + pltpu.roll(a, 7, 0), b + pltpu.roll(b, 1, 0))


def matvec(blocks_ref, position, vector, row):
    result = []
    for group in range(blocks_ref.shape[1] // 8):
        parts = []
        for k in range(8):
            terms = blocks_ref[position, group * 8 + k].astype(F32) * vector
            total = terms[0:8]
            for j in (*range(16, FEATURES, 16), *range(8, FEATURES, 16)):
                total = total + terms[j : j + 8]
            parts.append(total)
        result.append(fold_sublanes(parts, row))
    return jnp.concatenate(result, axis=0)


def sublane_ids():
    return lax.broadcasted_iota(jnp.int32, (8, LINES), 0)


def columns(table):
    padded = jnp.concatenate([table, jnp.full((16 - SLOTS, PEERS), -1, jnp.int32)], axis=0)
    return jnp.transpose(padded)


def one_hot(index, first):
    place = lax.broadcasted_iota(jnp.int32, (PEERS, CELLS), 1)
    return jnp.concatenate(
        [
            jnp.where(index[:, 2 * pair + first : 2 * pair + first + 1] == place, 1.0, 0.0).astype(BF16)
            for pair in range(PAIRS)
        ],
        axis=0,
    )


def across(a, b):
    return lax.dot_general(a, b, (((1,), (1,)), ((), ())), preferred_element_type=F32)


def down(a, b):
    return lax.dot_general(a, b, (((0,), (0,)), ((), ())), preferred_element_type=F32)


def swap(x):
    return pltpu.roll(x, SIDE, 1)


def left(rows):
    return lax.broadcasted_iota(jnp.int32, (rows, LANES), 1) < SIDE


def spread(rows, odd, extra):
    parts = [jnp.zeros((MAIN, CELLS), BF16), jnp.zeros((TAIL, CELLS), BF16)]
    at = slice(None, None, -1) if odd else slice(None)
    main = [rows[:MAIN], parts[0]][at]
    tail = [rows[MAIN:], parts[1]][at]
    if extra is None:
        note = parts[1]
    else:
        place = lax.broadcasted_iota(jnp.int32, (TAIL, CELLS), 0)
        note = jnp.where(place == odd, extra, 0.0).astype(BF16)
    rest = jnp.zeros((128 - 3 * TAIL, CELLS), BF16)
    return jnp.concatenate([*main, *tail, note, rest], axis=0)


def pack(pieces, hots, store, extra=None):
    packed = 0.0
    for odd, hot in enumerate(hots):
        for k, piece in enumerate(pieces):
            packed = packed + across(hot, spread(piece, odd, None if k else extra))
    lane = lax.broadcasted_iota(jnp.int32, (PEERS, LANES), 1)
    tails = []
    notes = 0.0
    for pair in range(PAIRS):
        rows = packed[pair * PEERS : (pair + 1) * PEERS]
        store(pair, rows[:, :128])
        tail = rows[:, 128:]
        if extra is not None:
            notes = notes + pltpu.roll(jnp.where(lane < 2 * TAIL, 0.0, tail), 2 * TAIL + 2 * pair, 1)
            tail = jnp.where(lane < 2 * TAIL, tail, 0.0)
        shift = 2 * TAIL * (pair % 4)
        tails.append(pltpu.roll(tail, shift, 1) if shift else tail)
    store(6, tails[0] + tails[1] + tails[2] + tails[3])
    store(7, tails[4] + tails[5] + notes)


def unpack(load, hots, pieces, noted=False):
    lane = lax.broadcasted_iota(jnp.int32, (PEERS, LANES), 1)
    last = (load(6), load(7))
    total = 0.0
    for odd in range(2):
        slots = []
        for pair in range(PAIRS):
            rows = load(pair)
            if odd:
                rows = pltpu.roll(rows, MAIN, 1)
            shift = (MAIN - 2 * TAIL * (pair % 4) - TAIL * odd) % LANES
            tail = last[pair // 4]
            tail = pltpu.roll(tail, shift, 1) if shift else tail
            note = 0.0
            if noted:
                note = pltpu.roll(last[1], FEATURES - MAIN - 2 * pair - odd, 1)
                note = jnp.where(lane == FEATURES, note, 0.0)
            slots.append(jnp.where(lane < MAIN, rows, jnp.where(lane < FEATURES, tail, note)))
        slots = jnp.concatenate(slots, axis=0)
        hot = hots[odd]
        for _ in range(pieces):
            part = slots.astype(BF16)
            total = total + down(part, hot)
            slots = slots - part.astype(F32)
    if noted:
        return total[:FEATURES], total[FEATURES : FEATURES + 8]
    return total[:FEATURES]


def pack_rows_kernel(rows_hbm, send_ref, out_ref, wide, rows_ref, sem):
    copy = pltpu.make_async_copy(rows_hbm, rows_ref, sem)
    copy.start()

    def store(r, block):
        wide[pl.ds(r, PEERS, stride=ROWS), :] = block

    index = columns(send_ref[...].reshape(SLOTS, PEERS))
    hots = one_hot(index, 0), one_hot(index, 1)
    copy.wait()
    pack([rows_ref[...]], hots, store)
    out_ref[...] = wide[...].astype(BF16)


def bundle_kernel(
    coupling_hbm, inverses_hbm, bundle_a_hbm, bundle_b_hbm, near_ref,
    whole, bundle_a, bundle_b, sems, near_sem,
):
    fetch, put_a, put_b = [
        [pltpu.make_async_copy(src.at[p], dst.at[p], sems.at[k, p]) for p in range(SEGMENT)]
        for k, (src, dst) in enumerate(
            ((coupling_hbm, whole), (bundle_a, bundle_a_hbm), (bundle_b, bundle_b_hbm))
        )
    ]
    for copy in fetch:
        copy.start()
    near = pltpu.make_async_copy(inverses_hbm.at[pl.ds(0, NEAR)], near_ref, near_sem)
    near.start()
    on_left = left(FEATURES)
    for p in range(SEGMENT):
        fetch[p].wait()

        @pl.loop(0, HALF // 8)
        def _(block):
            for k in range(8):
                low = whole[p, block * 16 + k]
                high = whole[p, block * 16 + 8 + k].astype(F32)
                high = jnp.concatenate(
                    [swap(high[j * 8 : j * 8 + 8]) for i in range(HALF // 8) for j in (2 * i + 1, 2 * i)],
                    axis=0,
                ).astype(BF16)
                bundle_a[p, block * 8 + k] = jnp.where(on_left, low, high)
                bundle_b[p, block * 8 + k] = jnp.where(on_left, high, low)

        put_a[p].start()
        put_b[p].start()
    for copy in put_a + put_b:
        copy.wait()
    near.wait()


def blocks8(x, odd):
    return jnp.concatenate([x[j * 8 : j * 8 + 8] for j in range(odd, FEATURES // 8, 2)], axis=0)


def move(coupling_ref, at, forcing, state):
    own = [state[j : j + 8] for j in range(0, HALF, 8)]
    both = jnp.concatenate([x for block in own for x in (block, swap(block))], axis=0)
    return forcing + matvec(coupling_ref, at, both, sublane_ids())


def advance(coupling_ref, forcing_ref, first, state, record=None):
    def step(position, state):
        if callable(first):
            first(position)
        state = move(coupling_ref, position, forcing_ref[position], state)
        if record is not None:
            record[position] = state
        return state

    if callable(first):
        return lax.fori_loop(1, SEGMENT, step, state)
    return lax.fori_loop(first, SEGMENT, step, state, unroll=2 if first == 0 else True)


def forcing_kernel(
    arrived_ref, cells_ref, counts_ref, near_ref, inverses_hbm, bundle_hbm,
    forcing_a, forcing_b, bundle_ref, end_ref,
    wide, lines, inverses_ref, sems, bundle_sems,
):
    def copy(p):
        return pltpu.make_async_copy(inverses_hbm.at[p], inverses_ref.at[p], sems.at[p])

    def bundle_copy(p):
        return pltpu.make_async_copy(bundle_hbm.at[p], bundle_ref.at[p], bundle_sems.at[p])

    for p in range(NEAR, SEGMENT):
        copy(p).start()
    wide[...] = arrived_ref[...].astype(F32)
    slot = lax.broadcasted_iota(jnp.int32, (SLOTS, PEERS), 0)
    index = columns(jnp.where(slot < counts_ref[...], cells_ref[...].reshape(SLOTS, PEERS), -1))
    hots = one_hot(index, 0), one_hot(index, 1)
    found = unpack(lambda r: wide[pl.ds(r, PEERS, stride=ROWS), :], hots, 1)
    for p in range(SEGMENT):
        lines[p] = found[:, p * LINES : (p + 1) * LINES]
    row = sublane_ids()
    on_left = left(HALF)

    def force(p, blocks_ref):
        forcing = matvec(blocks_ref, p, lines[p], row)
        low, high = blocks8(forcing, 0), swap(blocks8(forcing, 1))
        forcing_a[p] = jnp.where(on_left, low, high)
        forcing_b[p] = jnp.where(on_left, high, low)

    @pl.loop(0, NEAR)
    def _(p):
        bundle_copy(p + 1).start()
        force(p, near_ref)

    @pl.loop(NEAR, SEGMENT)
    def _(p):
        copy(p).wait()

        @pl.when(p + 1 < SEGMENT)
        def _():
            bundle_copy(p + 1).start()

        force(p, inverses_ref)

    end_ref[...] = advance(
        bundle_ref, forcing_a, lambda p: bundle_copy(p).wait(), forcing_a[0]
    )


def hots_kernel(cells_ref, counts_ref, even_ref, odd_ref):
    slot = lax.broadcasted_iota(jnp.int32, (SLOTS, PEERS), 0)
    index = columns(jnp.where(slot < counts_ref[...], cells_ref[...].reshape(SLOTS, PEERS), -1))
    even_ref[...] = one_hot(index, 0)
    odd_ref[...] = one_hot(index, 1)


def here(hop):
    return lax.axis_index("circ") == hop % N_CIRC


def first_hop_kernel(
    bundle_a_hbm, bundle_b_hbm, forcing_ref, end_ref, head_ref, bundle_ref, sems, head_sem
):
    def copy(p):
        return pltpu.make_async_copy(bundle_b_hbm.at[p], bundle_ref.at[p], sems.at[p])

    for p in (*range(1, SEGMENT), 0):
        copy(p).start()
    head = pltpu.make_async_copy(bundle_a_hbm.at[pl.ds(0, 1)], head_ref, head_sem)
    head.start()
    end_ref[...] = advance(bundle_ref, forcing_ref, lambda p: copy(p).wait(), forcing_ref[0])
    copy(0).wait()
    head.wait()


def widen_kernel(after_ref, *refs):
    *heads, bundle_ref, wide_ref = refs

    def widen(p, from_ref, at):
        @pl.loop(0, HALF, unroll=8)
        def _(i):
            wide_ref[p, i] = from_ref[at, i].astype(F32)

    if heads:
        widen(0, heads[0], 0)

    @pl.loop(len(heads), SEGMENT)
    def _(p):
        widen(p, bundle_ref, p)


def second_hop_kernel(state_ref, head_ref, coupling_ref, forcing_ref, end_ref):
    @pl.when(here(1))
    def _():
        state = move(head_ref, 0, forcing_ref[0], state_ref[...])
        end_ref[...] = advance(coupling_ref, forcing_ref, 1, state)


def hop_kernel(hop, state_ref, coupling_ref, forcing_ref, end_ref):
    @pl.when(here(hop))
    def _():
        end_ref[...] = advance(coupling_ref, forcing_ref, 0, state_ref[...])


def final_kernel(*refs):
    *state_refs, coupling_ref, forcing_ref, solved_ref = refs
    state = state_refs[0][...]
    for ref in state_refs[1:]:
        state = state + ref[...]
    advance(coupling_ref, forcing_ref, 0, state, solved_ref)


def half_power(exponent):
    return jnp.exp2(0.5 * exponent)


def return_pack_kernel(solved_a, solved_b, even_ref, odd_ref, out_ref, wide):
    def store(r, block):
        wide[pl.ds(r, PEERS, stride=ROWS), :] = block

    on_left = left(HALF)
    cells = []
    for position in range(SEGMENT):
        a, b = solved_a[position], solved_b[position]
        low = jnp.where(on_left, a, b)
        high = swap(jnp.where(on_left, b, a))
        blocks = [x[j : j + 8] for j in range(0, HALF, 8) for x in (low, high)]
        cells.append(jnp.concatenate(blocks, axis=0))
    rest = jnp.concatenate(cells, axis=1)
    largest = jnp.max(jnp.abs(rest), axis=0, keepdims=True)
    exponent = jnp.ceil(jnp.log2(jnp.maximum(largest, SMALLEST)))
    shrink = half_power(-exponent)
    whole = jnp.floor(rest * shrink * shrink * STEPS + 0.5)
    high = whole.astype(BF16)
    low = (whole - high.astype(F32)).astype(BF16)
    pack([high, low], (even_ref[...], odd_ref[...]), store, exponent)
    out_ref[...] = wide[...].astype(jnp.int32).astype(jnp.int16)


def return_kernel(arrived_ref, send_ref, out_ref, wide):
    wide[...] = arrived_ref[...].astype(jnp.int32).astype(F32)
    index = columns(send_ref[...].reshape(SLOTS, PEERS))
    whole, exponent = unpack(
        lambda r: wide[pl.ds(r, PEERS, stride=ROWS), :],
        (one_hot(index, 0), one_hot(index, 1)),
        2,
        True,
    )
    grow = half_power(exponent[:1])
    out_ref[...] = whole * (1.0 / STEPS) * grow * grow


def vmem(x):
    return pltpu.with_memory_space_constraint(x, pltpu.VMEM)


def hbm(x):
    return pltpu.with_memory_space_constraint(x, pltpu.HBM)


def exchange(rows):
    blocks = rows.reshape(PEERS, ROWS, 128)
    moved = lax.all_to_all(blocks, ("circ", "span"), split_axis=0, concat_axis=0, tiled=True)
    return moved.reshape(PEERS * ROWS, 128)


def local(elem_rows, coupling, inverses, send_rows, recv_cells, slot_counts):
    send = jnp.transpose(send_rows, (2, 0, 1))
    cells = jnp.transpose(recv_cells, (2, 0, 1))
    packed_rows = (PEERS * ROWS, LANES)
    hot_shape = jax.ShapeDtypeStruct((PAIRS * PEERS, CELLS), BF16)
    bundle_shape = jax.ShapeDtypeStruct((SEGMENT, HALF, FEATURES, LANES), BF16)
    state_shape = jax.ShapeDtypeStruct((HALF, LANES), F32)
    forcing_shape = jax.ShapeDtypeStruct((SEGMENT, HALF, LANES), F32)
    in_hbm = pl.BlockSpec(memory_space=pltpu.HBM)
    outgoing = pl.pallas_call(
        pack_rows_kernel,
        out_shape=jax.ShapeDtypeStruct(packed_rows, BF16),
        in_specs=[in_hbm, IN_VMEM],
        out_specs=IN_VMEM,
        scratch_shapes=[
            pltpu.VMEM(packed_rows, F32),
            pltpu.VMEM(elem_rows.shape, BF16),
            pltpu.SemaphoreType.DMA,
        ],
        compiler_params=params(16),
        name="pack_rows",
    )(hbm(elem_rows), send)
    arrived = exchange(outgoing)
    *bundles, near = pl.pallas_call(
        bundle_kernel,
        out_shape=[pltpu.HBM(bundle_shape.shape, BF16)] * 2
        + [jax.ShapeDtypeStruct((NEAR, *inverses.shape[1:]), BF16)],
        in_specs=[in_hbm] * 2,
        out_specs=[in_hbm] * 2 + [IN_VMEM],
        scratch_shapes=[
            pltpu.VMEM(coupling.shape, BF16),
            pltpu.VMEM(bundle_shape.shape, BF16),
            pltpu.VMEM(bundle_shape.shape, BF16),
            pltpu.SemaphoreType.DMA((3, SEGMENT)),
            pltpu.SemaphoreType.DMA,
        ],
        compiler_params=params(32),
        cost_estimate=pl.CostEstimate(flops=0, bytes_accessed=4 * coupling.size, transcendentals=0),
        name="bundle",
    )(hbm(coupling), hbm(inverses))
    *forcings, bundle_a, end_a = pl.pallas_call(
        forcing_kernel,
        out_shape=[forcing_shape] * 2 + [bundle_shape, state_shape],
        in_specs=[IN_VMEM] * 4 + [in_hbm] * 2,
        out_specs=[IN_VMEM] * 4,
        scratch_shapes=[
            pltpu.VMEM(packed_rows, F32),
            pltpu.VMEM((SEGMENT, FEATURES, LINES), F32),
            pltpu.VMEM(inverses.shape, BF16),
            pltpu.SemaphoreType.DMA((SEGMENT,)),
            pltpu.SemaphoreType.DMA((SEGMENT,)),
        ],
        compiler_params=params(24),
        name="forcing",
    )(arrived, cells, slot_counts, vmem(near), hbm(inverses), hbm(bundles[0]))
    forcings = [vmem(forcing) for forcing in forcings]
    end_b, head_a, bundle_b = pl.pallas_call(
        first_hop_kernel,
        out_shape=[
            state_shape,
            jax.ShapeDtypeStruct((1, *bundle_shape.shape[1:]), BF16),
            bundle_shape,
        ],
        in_specs=[in_hbm, in_hbm, IN_VMEM],
        out_specs=[IN_VMEM] * 3,
        scratch_shapes=[pltpu.SemaphoreType.DMA((SEGMENT,)), pltpu.SemaphoreType.DMA],
        compiler_params=params(8),
        name="first_hop",
    )(hbm(bundles[0]), hbm(bundles[1]), forcings[1])
    narrow = [[vmem(head_a), vmem(bundle_a)], [vmem(bundle_b)]]
    sweep_cost = pl.CostEstimate(
        flops=2 * 10**6, bytes_accessed=2 * bundle_shape.size, transcendentals=0
    )

    def sweep(kernel, states, blocks, forcing, shape, name):
        operands = [*states, *blocks, forcing]
        return pl.pallas_call(
            kernel,
            out_shape=shape,
            in_specs=[IN_VMEM] * len(operands),
            out_specs=IN_VMEM,
            compiler_params=params(8),
            cost_estimate=sweep_cost,
            name=name,
        )(*operands)

    def widen(after, blocks):
        return vmem(
            pl.pallas_call(
                widen_kernel,
                out_shape=jax.ShapeDtypeStruct(bundle_shape.shape, F32),
                in_specs=[IN_VMEM] * (1 + len(blocks)),
                out_specs=IN_VMEM,
                compiler_params=params(4),
                cost_estimate=sweep_cost,
                name="widen",
            )(after, *blocks)
        )

    cells, counts, _ = lax.optimization_barrier((cells, slot_counts, end_b))
    even, odd = pl.pallas_call(
        hots_kernel,
        out_shape=[hot_shape] * 2,
        in_specs=[IN_VMEM] * 2,
        out_specs=[IN_VMEM] * 2,
        compiler_params=params(8),
        name="hots",
    )(cells, counts)
    arrivals = ([], [])
    blocks = narrow
    for hop in range(2 * N_CIRC - 1):
        pair = (hop % N_CIRC, (hop + 1) % N_CIRC)
        for side in range(2):
            end = (end_a, end_b)[side]
            if hop:
                kernel = functools.partial(hop_kernel, hop)
                if hop == 1 and side == 0:
                    kernel = second_hop_kernel
                end = sweep(
                    kernel, arrivals[side][-1:], blocks[side], forcings[side], state_shape, "hop_" + "ab"[side]
                )
            arrivals[side].append(lax.ppermute(end, "circ", [pair]))
        if hop == 1:
            blocks = [[widen(end, part)] for part in narrow]
    solved = [
        sweep(
            final_kernel, arrivals[side][N_CIRC - 1 :], blocks[side], forcings[side], forcing_shape, "final_" + "ab"[side]
        )
        for side in range(2)
    ]

    returning = pl.pallas_call(
        return_pack_kernel,
        out_shape=jax.ShapeDtypeStruct(packed_rows, jnp.int16),
        in_specs=[IN_VMEM] * 4,
        out_specs=IN_VMEM,
        scratch_shapes=[pltpu.VMEM(packed_rows, F32)],
        compiler_params=params(16),
        name="return_pack",
    )(*solved, vmem(even), vmem(odd))
    returned = exchange(returning)
    return pl.pallas_call(
        return_kernel,
        out_shape=jax.ShapeDtypeStruct((FEATURES, CELLS), F32),
        in_specs=[IN_VMEM] * 2,
        out_specs=IN_VMEM,
        scratch_shapes=[pltpu.VMEM(packed_rows, F32)],
        compiler_params=params(16),
        name="return_rows",
    )(returned, send)


def solution(mesh):
    return jax.shard_map(
        local,
        mesh=mesh,
        in_specs=(
            P(None, ("circ", "span")),
            P("circ", None, None, "span"),
            P("circ", None, None, "span"),
            P(("circ", "span"), None, None),
            P(("circ", "span"), None, None),
            P(("circ", "span"), None),
        ),
        out_specs=P(None, ("circ", "span")),
        check_vma=False,
    )
```

```python
import functools

import jax
import jax.numpy as jnp
from jax import lax
from jax.experimental import pallas as pl
from jax.experimental.pallas import tpu as pltpu
from jax.sharding import PartitionSpec as P

FEATURES = 80
SEGMENT = 6
LINES = 128
CELLS = SEGMENT * LINES
PEERS = 128
SLOTS = 12
PAIRS = SLOTS // 2
ROWS = 8
MAIN = 64
TAIL = FEATURES - MAIN
N_CIRC = 8
STEPS = 32000.0
SMALLEST = 2.0**-100
NEAR = 2
HALF = FEATURES // 2
LANES = 128
SIDE = LANES // 2

IN_VMEM = pl.BlockSpec(memory_space=pltpu.VMEM)
F32 = jnp.float32
BF16 = jnp.bfloat16


def params(megabytes):
    return pltpu.CompilerParams(vmem_limit_bytes=megabytes * 2**20)


def fold_sublanes(parts, row):
    upper = row < 4
    fours = []
    for k in range(4):
        a, b = parts[k], parts[k + 4]
        fours.append(jnp.where(upper, a, b) + pltpu.roll(jnp.where(upper, b, a), 4, 0))
    even_pair = (row & 2) == 0
    twos = []
    for k in range(2):
        a, b = fours[k], fours[k + 2]
        twos.append(jnp.where(even_pair, a + pltpu.roll(a, 6, 0), b + pltpu.roll(b, 2, 0)))
    even = (row & 1) == 0
    a, b = twos
    return jnp.where(even, a + pltpu.roll(a, 7, 0), b + pltpu.roll(b, 1, 0))


def matvec(blocks_ref, position, vector, row):
    result = []
    for group in range(blocks_ref.shape[1] // 8):
        parts = []
        for k in range(8):
            terms = blocks_ref[position, group * 8 + k].astype(F32) * vector
            total = terms[0:8]
            for j in (*range(16, FEATURES, 16), *range(8, FEATURES, 16)):
                total = total + terms[j : j + 8]
            parts.append(total)
        result.append(fold_sublanes(parts, row))
    return jnp.concatenate(result, axis=0)


def sublane_ids():
    return lax.broadcasted_iota(jnp.int32, (8, LINES), 0)


def columns(table):
    padded = jnp.concatenate([table, jnp.full((16 - SLOTS, PEERS), -1, jnp.int32)], axis=0)
    return jnp.transpose(padded)


def one_hot(index, first):
    place = lax.broadcasted_iota(jnp.int32, (PEERS, CELLS), 1)
    return jnp.concatenate(
        [
            jnp.where(index[:, 2 * pair + first : 2 * pair + first + 1] == place, 1.0, 0.0).astype(BF16)
            for pair in range(PAIRS)
        ],
        axis=0,
    )


def across(a, b):
    return lax.dot_general(a, b, (((1,), (1,)), ((), ())), preferred_element_type=F32)


def down(a, b):
    return lax.dot_general(a, b, (((0,), (0,)), ((), ())), preferred_element_type=F32)


def swap(x):
    return pltpu.roll(x, SIDE, 1)


def left(rows):
    return lax.broadcasted_iota(jnp.int32, (rows, LANES), 1) < SIDE


def spread(rows, odd, extra):
    parts = [jnp.zeros((MAIN, CELLS), BF16), jnp.zeros((TAIL, CELLS), BF16)]
    at = slice(None, None, -1) if odd else slice(None)
    main = [rows[:MAIN], parts[0]][at]
    tail = [rows[MAIN:], parts[1]][at]
    if extra is None:
        note = parts[1]
    else:
        place = lax.broadcasted_iota(jnp.int32, (TAIL, CELLS), 0)
        note = jnp.where(place == odd, extra, 0.0).astype(BF16)
    rest = jnp.zeros((128 - 3 * TAIL, CELLS), BF16)
    return jnp.concatenate([*main, *tail, note, rest], axis=0)


def pack(pieces, hots, store, extra=None):
    packed = 0.0
    for odd, hot in enumerate(hots):
        for k, piece in enumerate(pieces):
            packed = packed + across(hot, spread(piece, odd, None if k else extra))
    lane = lax.broadcasted_iota(jnp.int32, (PEERS, LANES), 1)
    tails = []
    notes = 0.0
    for pair in range(PAIRS):
        rows = packed[pair * PEERS : (pair + 1) * PEERS]
        store(pair, rows[:, :128])
        tail = rows[:, 128:]
        if extra is not None:
            notes = notes + pltpu.roll(jnp.where(lane < 2 * TAIL, 0.0, tail), 2 * TAIL + 2 * pair, 1)
            tail = jnp.where(lane < 2 * TAIL, tail, 0.0)
        shift = 2 * TAIL * (pair % 4)
        tails.append(pltpu.roll(tail, shift, 1) if shift else tail)
    store(6, tails[0] + tails[1] + tails[2] + tails[3])
    store(7, tails[4] + tails[5] + notes)


def unpack(load, hots, pieces, noted=False):
    lane = lax.broadcasted_iota(jnp.int32, (PEERS, LANES), 1)
    last = (load(6), load(7))
    total = 0.0
    for odd in range(2):
        slots = []
        for pair in range(PAIRS):
            rows = load(pair)
            if odd:
                rows = pltpu.roll(rows, MAIN, 1)
            shift = (MAIN - 2 * TAIL * (pair % 4) - TAIL * odd) % LANES
            tail = last[pair // 4]
            tail = pltpu.roll(tail, shift, 1) if shift else tail
            note = 0.0
            if noted:
                note = pltpu.roll(last[1], FEATURES - MAIN - 2 * pair - odd, 1)
                note = jnp.where(lane == FEATURES, note, 0.0)
            slots.append(jnp.where(lane < MAIN, rows, jnp.where(lane < FEATURES, tail, note)))
        slots = jnp.concatenate(slots, axis=0)
        hot = hots[odd]
        for _ in range(pieces):
            part = slots.astype(BF16)
            total = total + down(part, hot)
            slots = slots - part.astype(F32)
    if noted:
        return total[:FEATURES], total[FEATURES : FEATURES + 8]
    return total[:FEATURES]


def pack_rows_kernel(rows_hbm, send_ref, out_ref, wide, rows_ref, sem):
    copy = pltpu.make_async_copy(rows_hbm, rows_ref, sem)
    copy.start()

    def store(r, block):
        wide[pl.ds(r, PEERS, stride=ROWS), :] = block

    index = columns(send_ref[...].reshape(SLOTS, PEERS))
    hots = one_hot(index, 0), one_hot(index, 1)
    copy.wait()
    pack([rows_ref[...]], hots, store)
    out_ref[...] = wide[...].astype(BF16)


def bundle_rows(whole, bundle_a, bundle_b, p):
    on_left = left(FEATURES)

    @pl.loop(0, HALF // 8)
    def _(block):
        for k in range(8):
            low = whole[p, block * 16 + k]
            high = whole[p, block * 16 + 8 + k].astype(F32)
            high = jnp.concatenate(
                [swap(high[j * 8 : j * 8 + 8]) for i in range(HALF // 8) for j in (2 * i + 1, 2 * i)],
                axis=0,
            ).astype(BF16)
            bundle_a[p, block * 8 + k] = jnp.where(on_left, low, high)
            bundle_b[p, block * 8 + k] = jnp.where(on_left, high, low)


def bundle_kernel(
    coupling_hbm, inverses_hbm, bundle_a_hbm, bundle_b_hbm, near_ref,
    whole, bundle_a, bundle_b, sems, near_sem,
):
    fetch, put_a, put_b = [
        [pltpu.make_async_copy(src.at[p], dst.at[p], sems.at[k, p]) for p in range(SEGMENT)]
        for k, (src, dst) in enumerate(
            ((coupling_hbm, whole), (bundle_a, bundle_a_hbm), (bundle_b, bundle_b_hbm))
        )
    ]
    for copy in fetch[1:]:
        copy.start()
    near = pltpu.make_async_copy(inverses_hbm.at[pl.ds(0, NEAR)], near_ref, near_sem)
    near.start()
    for p in range(1, SEGMENT):
        fetch[p].wait()
        bundle_rows(whole, bundle_a, bundle_b, p)
        put_a[p].start()
        put_b[p].start()
    for copy in put_a[1:] + put_b[1:]:
        copy.wait()
    near.wait()


def blocks8(x, odd):
    return jnp.concatenate([x[j * 8 : j * 8 + 8] for j in range(odd, FEATURES // 8, 2)], axis=0)


def move(coupling_ref, at, forcing, state):
    own = [state[j : j + 8] for j in range(0, HALF, 8)]
    both = jnp.concatenate([x for block in own for x in (block, swap(block))], axis=0)
    return forcing + matvec(coupling_ref, at, both, sublane_ids())


def advance(coupling_ref, forcing_ref, first, state, record=None):
    def step(position, state):
        if callable(first):
            first(position)
        state = move(coupling_ref, position, forcing_ref[position], state)
        if record is not None:
            record[position] = state
        return state

    if callable(first):
        return lax.fori_loop(1, SEGMENT, step, state)
    return lax.fori_loop(first, SEGMENT, step, state, unroll=2 if first == 0 else True)


def forcing_kernel(
    arrived_ref, cells_ref, counts_ref, near_ref, inverses_hbm, bundle_hbm,
    forcing_a, forcing_b, bundle_ref, end_ref,
    wide, lines, inverses_ref, sems, bundle_sems,
):
    def copy(p):
        return pltpu.make_async_copy(inverses_hbm.at[p], inverses_ref.at[p], sems.at[p])

    def bundle_copy(p):
        return pltpu.make_async_copy(bundle_hbm.at[p], bundle_ref.at[p], bundle_sems.at[p])

    for p in range(NEAR, SEGMENT):
        copy(p).start()
    wide[...] = arrived_ref[...].astype(F32)
    slot = lax.broadcasted_iota(jnp.int32, (SLOTS, PEERS), 0)
    index = columns(jnp.where(slot < counts_ref[...], cells_ref[...].reshape(SLOTS, PEERS), -1))
    hots = one_hot(index, 0), one_hot(index, 1)
    found = unpack(lambda r: wide[pl.ds(r, PEERS, stride=ROWS), :], hots, 1)
    for p in range(SEGMENT):
        lines[p] = found[:, p * LINES : (p + 1) * LINES]
    row = sublane_ids()
    on_left = left(HALF)

    def force(p, blocks_ref):
        forcing = matvec(blocks_ref, p, lines[p], row)
        low, high = blocks8(forcing, 0), swap(blocks8(forcing, 1))
        forcing_a[p] = jnp.where(on_left, low, high)
        forcing_b[p] = jnp.where(on_left, high, low)

    @pl.loop(0, NEAR)
    def _(p):
        bundle_copy(p + 1).start()
        force(p, near_ref)

    @pl.loop(NEAR, SEGMENT)
    def _(p):
        copy(p).wait()

        @pl.when(p + 1 < SEGMENT)
        def _():
            bundle_copy(p + 1).start()

        force(p, inverses_ref)

    end_ref[...] = advance(
        bundle_ref, forcing_a, lambda p: bundle_copy(p).wait(), forcing_a[0]
    )


def hots_kernel(cells_ref, counts_ref, even_ref, odd_ref):
    slot = lax.broadcasted_iota(jnp.int32, (SLOTS, PEERS), 0)
    index = columns(jnp.where(slot < counts_ref[...], cells_ref[...].reshape(SLOTS, PEERS), -1))
    even_ref[...] = one_hot(index, 0)
    odd_ref[...] = one_hot(index, 1)


def here(hop):
    return lax.axis_index("circ") == hop % N_CIRC


def first_hop_kernel(bundle_hbm, forcing_ref, end_ref, bundle_ref, sems):
    def copy(p):
        return pltpu.make_async_copy(bundle_hbm.at[p], bundle_ref.at[p], sems.at[p])

    for p in range(1, SEGMENT):
        copy(p).start()
    end_ref[...] = advance(bundle_ref, forcing_ref, lambda p: copy(p).wait(), forcing_ref[0])


def heads_kernel(after_ref, coupling_hbm, head_a, head_b, whole, sem):
    head = pltpu.make_async_copy(coupling_hbm.at[pl.ds(0, 1)], whole, sem)
    head.start()
    head.wait()
    bundle_rows(whole, head_a, head_b, 0)


def widen_kernel(after_ref, *refs):
    *heads, bundle_ref, wide_ref = refs

    def widen(p, from_ref, at):
        @pl.loop(0, HALF, unroll=8)
        def _(i):
            wide_ref[p, i] = from_ref[at, i].astype(F32)

    if heads:
        widen(0, heads[0], 0)

    @pl.loop(len(heads), SEGMENT)
    def _(p):
        widen(p, bundle_ref, p)


def second_hop_kernel(state_ref, head_ref, coupling_ref, forcing_ref, end_ref):
    @pl.when(here(1))
    def _():
        state = move(head_ref, 0, forcing_ref[0], state_ref[...])
        end_ref[...] = advance(coupling_ref, forcing_ref, 1, state)


def hop_kernel(hop, state_ref, coupling_ref, forcing_ref, end_ref):
    @pl.when(here(hop))
    def _():
        end_ref[...] = advance(coupling_ref, forcing_ref, 0, state_ref[...])


def final_kernel(*refs):
    *state_refs, coupling_ref, forcing_ref, solved_ref = refs
    state = state_refs[0][...]
    for ref in state_refs[1:]:
        state = state + ref[...]
    advance(coupling_ref, forcing_ref, 0, state, solved_ref)


def half_power(exponent):
    return jnp.exp2(0.5 * exponent)


def return_pack_kernel(solved_a, solved_b, even_ref, odd_ref, out_ref, wide):
    def store(r, block):
        wide[pl.ds(r, PEERS, stride=ROWS), :] = block

    on_left = left(HALF)
    cells = []
    for position in range(SEGMENT):
        a, b = solved_a[position], solved_b[position]
        low = jnp.where(on_left, a, b)
        high = swap(jnp.where(on_left, b, a))
        blocks = [x[j : j + 8] for j in range(0, HALF, 8) for x in (low, high)]
        cells.append(jnp.concatenate(blocks, axis=0))
    rest = jnp.concatenate(cells, axis=1)
    largest = jnp.max(jnp.abs(rest), axis=0, keepdims=True)
    exponent = jnp.ceil(jnp.log2(jnp.maximum(largest, SMALLEST)))
    shrink = half_power(-exponent)
    whole = jnp.floor(rest * shrink * shrink * STEPS + 0.5)
    high = whole.astype(BF16)
    low = (whole - high.astype(F32)).astype(BF16)
    pack([high, low], (even_ref[...], odd_ref[...]), store, exponent)
    out_ref[...] = wide[...].astype(jnp.int32).astype(jnp.int16)


def return_kernel(arrived_ref, send_ref, out_ref, wide):
    wide[...] = arrived_ref[...].astype(jnp.int32).astype(F32)
    index = columns(send_ref[...].reshape(SLOTS, PEERS))
    whole, exponent = unpack(
        lambda r: wide[pl.ds(r, PEERS, stride=ROWS), :],
        (one_hot(index, 0), one_hot(index, 1)),
        2,
        True,
    )
    grow = half_power(exponent[:1])
    out_ref[...] = whole * (1.0 / STEPS) * grow * grow


def vmem(x):
    return pltpu.with_memory_space_constraint(x, pltpu.VMEM)


def hbm(x):
    return pltpu.with_memory_space_constraint(x, pltpu.HBM)


def exchange(rows):
    blocks = rows.reshape(PEERS, ROWS, 128)
    moved = lax.all_to_all(blocks, ("circ", "span"), split_axis=0, concat_axis=0, tiled=True)
    return moved.reshape(PEERS * ROWS, 128)


def local(elem_rows, coupling, inverses, send_rows, recv_cells, slot_counts):
    send = jnp.transpose(send_rows, (2, 0, 1))
    cells = jnp.transpose(recv_cells, (2, 0, 1))
    packed_rows = (PEERS * ROWS, LANES)
    hot_shape = jax.ShapeDtypeStruct((PAIRS * PEERS, CELLS), BF16)
    bundle_shape = jax.ShapeDtypeStruct((SEGMENT, HALF, FEATURES, LANES), BF16)
    state_shape = jax.ShapeDtypeStruct((HALF, LANES), F32)
    forcing_shape = jax.ShapeDtypeStruct((SEGMENT, HALF, LANES), F32)
    in_hbm = pl.BlockSpec(memory_space=pltpu.HBM)
    outgoing = pl.pallas_call(
        pack_rows_kernel,
        out_shape=jax.ShapeDtypeStruct(packed_rows, BF16),
        in_specs=[in_hbm, IN_VMEM],
        out_specs=IN_VMEM,
        scratch_shapes=[
            pltpu.VMEM(packed_rows, F32),
            pltpu.VMEM(elem_rows.shape, BF16),
            pltpu.SemaphoreType.DMA,
        ],
        compiler_params=params(16),
        name="pack_rows",
    )(hbm(elem_rows), send)
    arrived = exchange(outgoing)
    *bundles, near = pl.pallas_call(
        bundle_kernel,
        out_shape=[pltpu.HBM(bundle_shape.shape, BF16)] * 2
        + [jax.ShapeDtypeStruct((NEAR, *inverses.shape[1:]), BF16)],
        in_specs=[in_hbm] * 2,
        out_specs=[in_hbm] * 2 + [IN_VMEM],
        scratch_shapes=[
            pltpu.VMEM(coupling.shape, BF16),
            pltpu.VMEM(bundle_shape.shape, BF16),
            pltpu.VMEM(bundle_shape.shape, BF16),
            pltpu.SemaphoreType.DMA((3, SEGMENT)),
            pltpu.SemaphoreType.DMA,
        ],
        compiler_params=params(32),
        cost_estimate=pl.CostEstimate(flops=0, bytes_accessed=4 * coupling.size, transcendentals=0),
        name="bundle",
    )(hbm(coupling), hbm(inverses))
    *forcings, bundle_a, end_a = pl.pallas_call(
        forcing_kernel,
        out_shape=[forcing_shape] * 2 + [bundle_shape, state_shape],
        in_specs=[IN_VMEM] * 4 + [in_hbm] * 2,
        out_specs=[IN_VMEM] * 4,
        scratch_shapes=[
            pltpu.VMEM(packed_rows, F32),
            pltpu.VMEM((SEGMENT, FEATURES, LINES), F32),
            pltpu.VMEM(inverses.shape, BF16),
            pltpu.SemaphoreType.DMA((SEGMENT,)),
            pltpu.SemaphoreType.DMA((SEGMENT,)),
        ],
        compiler_params=params(24),
        name="forcing",
    )(arrived, cells, slot_counts, vmem(near), hbm(inverses), hbm(bundles[0]))
    forcings = [vmem(forcing) for forcing in forcings]
    head_shape = jax.ShapeDtypeStruct((1, *bundle_shape.shape[1:]), BF16)
    end_b, bundle_b = pl.pallas_call(
        first_hop_kernel,
        out_shape=[state_shape, bundle_shape],
        in_specs=[in_hbm, IN_VMEM],
        out_specs=[IN_VMEM] * 2,
        scratch_shapes=[pltpu.SemaphoreType.DMA((SEGMENT,))],
        compiler_params=params(8),
        name="first_hop",
    )(hbm(bundles[1]), forcings[1])
    head_a, head_b = pl.pallas_call(
        heads_kernel,
        out_shape=[head_shape, head_shape],
        in_specs=[IN_VMEM, in_hbm],
        out_specs=[IN_VMEM] * 2,
        scratch_shapes=[
            pltpu.VMEM((1, *coupling.shape[1:]), BF16),
            pltpu.SemaphoreType.DMA,
        ],
        compiler_params=params(8),
        cost_estimate=pl.CostEstimate(flops=10**6, bytes_accessed=4 * 10**6, transcendentals=0),
        name="heads",
    )(end_b, hbm(coupling))
    narrow = [[vmem(head_a), vmem(bundle_a)], [vmem(head_b), vmem(bundle_b)]]
    sweep_cost = pl.CostEstimate(
        flops=2 * 10**6, bytes_accessed=2 * bundle_shape.size, transcendentals=0
    )

    def sweep(kernel, states, blocks, forcing, shape, name):
        operands = [*states, *blocks, forcing]
        return pl.pallas_call(
            kernel,
            out_shape=shape,
            in_specs=[IN_VMEM] * len(operands),
            out_specs=IN_VMEM,
            compiler_params=params(8),
            cost_estimate=sweep_cost,
            name=name,
        )(*operands)

    def widen(after, blocks):
        return vmem(
            pl.pallas_call(
                widen_kernel,
                out_shape=jax.ShapeDtypeStruct(bundle_shape.shape, F32),
                in_specs=[IN_VMEM] * (1 + len(blocks)),
                out_specs=IN_VMEM,
                compiler_params=params(4),
                cost_estimate=sweep_cost,
                name="widen",
            )(after, *blocks)
        )

    cells, counts, _ = lax.optimization_barrier((cells, slot_counts, end_b))
    even, odd = pl.pallas_call(
        hots_kernel,
        out_shape=[hot_shape] * 2,
        in_specs=[IN_VMEM] * 2,
        out_specs=[IN_VMEM] * 2,
        compiler_params=params(8),
        name="hots",
    )(cells, counts)
    arrivals = ([], [])
    blocks = narrow
    for hop in range(2 * N_CIRC - 1):
        pair = (hop % N_CIRC, (hop + 1) % N_CIRC)
        for side in range(2):
            end = (end_a, end_b)[side]
            if hop:
                kernel = functools.partial(hop_kernel, hop)
                if hop == 1:
                    kernel = second_hop_kernel
                end = sweep(
                    kernel, arrivals[side][-1:], blocks[side], forcings[side], state_shape, "hop_" + "ab"[side]
                )
            arrivals[side].append(lax.ppermute(end, "circ", [pair]))
        if hop == 1:
            blocks = [[widen(end, part)] for part in narrow]
    solved = [
        sweep(
            final_kernel, arrivals[side][N_CIRC - 1 :], blocks[side], forcings[side], forcing_shape, "final_" + "ab"[side]
        )
        for side in range(2)
    ]

    returning = pl.pallas_call(
        return_pack_kernel,
        out_shape=jax.ShapeDtypeStruct(packed_rows, jnp.int16),
        in_specs=[IN_VMEM] * 4,
        out_specs=IN_VMEM,
        scratch_shapes=[pltpu.VMEM(packed_rows, F32)],
        compiler_params=params(16),
        name="return_pack",
    )(*solved, vmem(even), vmem(odd))
    returned = exchange(returning)
    return pl.pallas_call(
        return_kernel,
        out_shape=jax.ShapeDtypeStruct((FEATURES, CELLS), F32),
        in_specs=[IN_VMEM] * 2,
        out_specs=IN_VMEM,
        scratch_shapes=[pltpu.VMEM(packed_rows, F32)],
        compiler_params=params(16),
        name="return_rows",
    )(returned, send)


def solution(mesh):
    return jax.shard_map(
        local,
        mesh=mesh,
        in_specs=(
            P(None, ("circ", "span")),
            P("circ", None, None, "span"),
            P("circ", None, None, "span"),
            P(("circ", "span"), None, None),
            P(("circ", "span"), None, None),
            P(("circ", "span"), None),
        ),
        out_specs=P(None, ("circ", "span")),
        check_vma=False,
    )
```
